512 devices in a mesh: row: 16 (over x, y), col: 32 (over z, core).
Axes of the slice: x: 4, y: 4, z: 16, core: 2. Of those that a mesh axis runs over, the one named last changes fastest.
Arguments:
- heights: float32 [2048, 8192], P('row', 'col'), may hold values from -6 to 6
- albedo: float32 [2048, 8192], P('row', 'col'), may hold values from 0.5 to 1.5
- images: float32 [8, 2048, 8192], P(None, 'row', 'col'), may hold values from 0.2 to 1.2
- lights: float32 [8, 2], replicated, may hold values from -0.7 to 0.7
Outputs:
- solution: float32 [2048, 8192], P('row', 'col')
- residual: float32 [2048, 8192], P('row', 'col')
The draws below stay inside these ranges and needn't reach their ends.
All inputs are finite; a program needn't handle non-finite values.
Results may differ from the reference program's by a relative error of at most 0.0003.
Values sent between devices are 32-bit elements; how exact they have to be, the bound alone decides.
A program may use at most 64 MiB of HBM per device.

```python
import math
import jax
import jax.numpy as jnp

NIMG = 8
ITERS = 2
NX = 2048
NY = 8192


def shard_levels(own_key, extent, split, least, top_value):
    loudness, own = 1.0, jax.random.fold_in(own_key, 6)
    for dim, shards_of in split:
        steps = jnp.exp(jax.random.uniform(jax.random.fold_in(own, dim), (shards_of,), jnp.float32, least / len(split), top_value / len(split)))
        loudness = loudness * jnp.repeat(steps, extent[dim] // shards_of).reshape([-1 if axis == dim else 1 for axis in range(len(extent))])
    return loudness


def gaussian(key, dims, deviation, bound, split=(), held_as=jnp.bfloat16):
    entries = deviation * jax.random.normal(key, dims, jnp.float32)
    if split:
        entries = entries * shard_levels(key, dims, split, -0.22, 0.18)
    return jnp.clip(entries, -bound, bound).astype(held_as)


def setup_inputs(seed: int = 0) -> dict:
    key_list = jax.random.split(jax.random.key(seed), 5)
    return {
        "heights": gaussian(key_list[0], (NX, NY), 1.0, 6.0, ((0, 16), (1, 32)), jnp.float32),
        "albedo": jnp.clip(jnp.exp(math.log(1.5) - 1.0986123 * jax.random.uniform(key_list[1], (NX, NY), jnp.float32) ** shard_levels(key_list[1], (NX, NY), ((0, 16), (1, 32)), -0.2, 0.2)), 0.5, 1.5),
        "images": jnp.clip(0.2 + 1 * jax.random.uniform(key_list[2], (NIMG, NX, NY), jnp.float32) ** shard_levels(key_list[2], (NIMG, NX, NY), ((1, 16), (2, 32)), -0.2, 0.2), 0.2, 1.2),
        "lights": jnp.clip(jax.random.uniform(key_list[3], (NIMG, 2), jnp.float32, -0.7, 0.7), -0.7, 0.7),
    }


curvature_weight = 0.25
damping = 1.0

def diff_cols(field):
    padded = jnp.pad(field, ((1, 1), (1, 1)))
    return 0.5 * (padded[1:-1, 2:] - padded[1:-1, :-2])

def diff_rows(field):
    padded = jnp.pad(field, ((1, 1), (1, 1)))
    return 0.5 * (padded[2:, 1:-1] - padded[:-2, 1:-1])

def laplace(field):
    padded = jnp.pad(field, ((1, 1), (1, 1)))
    return padded[2:, 1:-1] + padded[:-2, 1:-1] + padded[1:-1, 2:] + padded[1:-1, :-2] - 4.0 * field

def reference(heights, albedo, images, lights):
    slope_x = diff_cols(heights)
    slope_y = diff_rows(heights)
    slant_sq = 1.0 + slope_x * slope_x + slope_y * slope_y
    slant_norm = jnp.sqrt(slant_sq)
    coef_xx = jnp.zeros_like(heights)
    coef_xy = jnp.zeros_like(heights)
    coef_yy = jnp.zeros_like(heights)
    flux_x = jnp.zeros_like(heights)
    flux_y = jnp.zeros_like(heights)
    for image_index in range(NIMG):
        light_x = lights[image_index, 0]
        light_y = lights[image_index, 1]
        norm_light = jnp.sqrt(1.0 + light_x * light_x + light_y * light_y)
        shading = albedo / (norm_light * slant_norm)
        facing = 1.0 - slope_x * light_x - slope_y * light_y
        mismatch = shading * facing - images[image_index]
        deriv_x = shading * (-light_x - facing * slope_x / slant_sq)
        deriv_y = shading * (-light_y - facing * slope_y / slant_sq)
        coef_xx = coef_xx + deriv_x * deriv_x
        coef_xy = coef_xy + deriv_x * deriv_y
        coef_yy = coef_yy + deriv_y * deriv_y
        flux_x = flux_x + deriv_x * mismatch
        flux_y = flux_y + deriv_y * mismatch
    rhs = diff_cols(flux_x) + diff_rows(flux_y) - curvature_weight * laplace(laplace(heights))

    def operate(field):
        grad_x = diff_cols(field)
        grad_y = diff_rows(field)
        weighted_x = coef_xx * grad_x + coef_xy * grad_y
        weighted_y = coef_xy * grad_x + coef_yy * grad_y
        return -(diff_cols(weighted_x) + diff_rows(weighted_y)) + curvature_weight * laplace(laplace(field)) + damping * field
    solution = jnp.zeros_like(rhs)
    residual = rhs
    direction = rhs
    norm_now = jnp.sum(residual * residual)
    for iteration in range(ITERS):
        applied = operate(direction)
        step_size = norm_now / jnp.sum(direction * applied)
        solution = solution + step_size * direction
        residual = residual - step_size * applied
        norm_next = jnp.sum(residual * residual)
        direction = residual + norm_next / norm_now * direction
        norm_now = norm_next
    return (solution, residual)
```

```python
import jax
import jax.numpy as jnp
from jax import lax
from jax.experimental import pallas as pl
from jax.experimental.pallas import tpu as pltpu
from jax.sharding import PartitionSpec as P

MESH = pl.DeviceIdType.MESH
F32 = jnp.float32
NIMG = 8
NR, NC = 16, 32
ROWS, COLS = 128, 256
TILES = ROWS // 8
NF = 5
TOP = 16
STRIDE = 12


def kernel(
    heights, albedo, images, lights, sol_out, res_out,
    fields, img, light, packs, strips, corners, coef, xs, yp, ym, vec_r, vec_u, vec_w, part, sums_row, sums_col,
    in_sem, img_sem, send_sem, recv_sem, ar_send, ar_recv,
):
    row, col = lax.axis_index("row"), lax.axis_index("col")

    def dev(dr, dc):
        return (lax.rem(row + (dr + NR), NR), lax.rem(col + (dc + NC), NC))

    loads = []
    for f, src in enumerate((heights, albedo)):
        for t in range(2):
            loads.append(
                pltpu.make_async_copy(src.at[:, pl.ds(128 * t, 128)], fields.at[f, t, pl.ds(TOP, ROWS), :], in_sem.at[2 * f + t])
            )
    load_light = pltpu.make_async_copy(lights, light, in_sem.at[4])
    load_img = [pltpu.make_async_copy(images.at[k], img.at[k], img_sem.at[k]) for k in range(NIMG)]
    load_light.start()
    for cp in load_img:
        cp.start()
    for cp in loads:
        cp.start()

    peers = {(a, b) for a in (-1, 0, 1) for b in (-1, 0, 1)} | {(d, 0) for d in range(NR)} | {(0, d) for d in range(NC)}
    peers = sorted({(a % NR, b % NC) for a, b in peers} - {(0, 0)})
    barrier = pltpu.get_barrier_semaphore()
    for p in peers:
        pl.semaphore_signal(barrier, inc=1, device_id=dev(*p), device_id_type=MESH)

    lane = lax.broadcasted_iota(jnp.int32, (8, 128), 1)
    zero = jnp.zeros((8, 128), F32)
    for t in range(3):
        for ref in (fields.at[0], yp, ym, vec_r, vec_u):
            ref[t, pl.ds(0, 8), :] = zero
            ref[t, pl.ds(ROWS + 24, 8), :] = zero

    load_light.wait()
    lx, ly = light[0:1, :], light[1:2, :]
    inv_sq = 1.0 / (1.0 + lx * lx + ly * ly)
    inv_norm = jnp.sqrt(inv_sq)

    def over_images(x):
        return jnp.broadcast_to(jnp.sum(x, axis=1, keepdims=True), (8, 128))

    m00, m10, m01 = over_images(inv_sq), over_images(inv_sq * lx), over_images(inv_sq * ly)
    m20, m11, m02 = over_images(inv_sq * lx * lx), over_images(inv_sq * lx * ly), over_images(inv_sq * ly * ly)
    weights = [
        [jnp.broadcast_to(w[:, k : k + 1], (8, 128)) for w in (inv_norm, inv_norm * lx, inv_norm * ly)] for k in range(NIMG)
    ]

    for cp in load_img:
        cp.wait()

    def image_sums(i, carry):
        at = pl.ds(pl.multiple_of(8 * i, 8), 8)
        to = pl.ds(pl.multiple_of(8 * i + TOP, 8), 8)
        for t in range(2):
            acc = [zero, zero, zero]
            for k in range(NIMG):
                v = img[k, at, pl.ds(128 * t, 128)]
                acc = [acc[j] + weights[k][j] * v for j in range(3)]
            for j in range(3):
                fields[2 + j, t, to, :] = acc[j]
        return carry

    lax.fori_loop(0, TILES, image_sums, 0, unroll=2)
    for cp in loads:
        cp.wait()

    shifts = [(64 * g + STRIDE * f, g, f) for g in range(2) for f in range(NF)]

    def pack(j, carry):
        left, right, first = zero, zero, None
        for s, g, f in shifts:
            at = pl.ds(pl.multiple_of(8 * j + (64 * g + TOP), 8), 8)
            a, b = fields[f, 0, at, :], fields[f, 1, at, :]
            if s:
                a, b = pltpu.roll(a, s, 1), pltpu.roll(b, s, 1)
                left = jnp.where(lane >= s, a, left)
                right = jnp.where(lane >= s - 6, b, right)
            else:
                left, right, first = a, b, b
        to = pl.ds(pl.multiple_of(8 * j, 8), 8)
        packs[0, to, :] = left
        packs[1, to, :] = jnp.where(lane >= 122, first, right)
        return carry

    lax.fori_loop(0, 8, pack, 0, unroll=2)

    pl.semaphore_wait(barrier, len(peers))
    first8, last8 = pl.ds(0, 8), pl.ds(56, 8)
    moves = [
        (packs.at[0, first8, :], corners.at[1, 0], (-1, -1)),
        (packs.at[1, first8, :], corners.at[1, 1], (-1, 1)),
        (packs.at[0, last8, :], corners.at[0, 0], (1, -1)),
        (packs.at[1, last8, :], corners.at[0, 1], (1, 1)),
        (fields.at[:, pl.ds(0, 2), pl.ds(TOP, 8), :], fields.at[:, pl.ds(0, 2), pl.ds(TOP + ROWS, 8), :], (-1, 0)),
        (fields.at[:, pl.ds(0, 2), pl.ds(TOP + ROWS - 8, 8), :], fields.at[:, pl.ds(0, 2), pl.ds(TOP - 8, 8), :], (1, 0)),
        (packs.at[0], strips.at[0], (0, -1)),
        (packs.at[1], strips.at[1], (0, 1)),
    ]
    copies = [
        pltpu.make_async_remote_copy(
            src_ref=src, dst_ref=dst, send_sem=send_sem.at[n], recv_sem=recv_sem.at[n], device_id=dev(*to), device_id_type=MESH
        )
        for n, (src, dst, to) in enumerate(moves)
    ]
    for cp in copies:
        cp.start()
    for cp in copies:
        cp.wait()

    above = jnp.where(row > 0, 1.0, 0.0).astype(F32)
    below = jnp.where(row < NR - 1, 1.0, 0.0).astype(F32)
    before = jnp.where(col > 0, 1.0, 0.0).astype(F32)
    after = jnp.where(col < NC - 1, 1.0, 0.0).astype(F32)
    side_mask = jnp.where(lane < 64, after, before)

    def masks(e):
        m = jnp.where(e == 0, above, jnp.where(e == TILES + 1, below, 1.0))
        return (m, m, m * side_mask)

    in_group = lane & 63
    from_right = in_group < 6
    for f in range(1, NF):
        from_right = from_right | ((in_group >= STRIDE * f) & (in_group < STRIDE * f + 6))

    def side(merged, g, f, at, mask):
        s = 64 * g + STRIDE * f
        v = pltpu.roll(merged, 128 - s, 1) if s else merged
        fields[f, 2, at, :] = v * mask if f < 2 else v

    def unpack(j, carry):
        at = pl.ds(pl.multiple_of(8 * j, 8), 8)
        merged = jnp.where(from_right, strips[0, at, :], strips[1, at, :])
        for s, g, f in shifts:
            side(merged, g, f, pl.ds(pl.multiple_of(8 * j + (64 * g + TOP), 8), 8), side_mask)
        return carry

    lax.fori_loop(0, 8, unpack, 0, unroll=2)
    for b, g, start, ok in ((0, 1, TOP - 8, above), (1, 0, TOP + ROWS, below)):
        merged = jnp.where(from_right, corners[b, 0], corners[b, 1])
        at = pl.ds(start, 8)
        for f in range(NF):
            side(merged, g, f, at, side_mask * ok)
        for f in range(2):
            for t in range(2):
                fields[f, t, at, :] = fields[f, t, at, :] * ok

    is_last, is_first = lane == 127, lane == 0

    def nexts(v):
        r = [pltpu.roll(x, 127, 1) for x in v]
        return [jnp.where(is_last, r[(t + 1) % 3], r[t]) for t in range(3)]

    def prevs(v):
        r = [pltpu.roll(x, 1, 1) for x in v]
        return [jnp.where(is_first, r[(t + 2) % 3], r[t]) for t in range(3)]

    def scatter(e, q, hx, hy):
        n = nexts([q[t] - hx[t] for t in range(3)])
        p = prevs([q[t] + hx[t] for t in range(3)])
        at, to = pl.ds(pl.multiple_of(8 * e, 8), 8), pl.ds(pl.multiple_of(8 * e + 8, 8), 8)
        for t in range(3):
            xs[t, at, :] = n[t] + p[t] - 4.0 * q[t]
            yp[t, to, :] = q[t] - hy[t]
            ym[t, to, :] = q[t] + hy[t]

    def stencil(ref, e):
        base = 8 * e + 8
        v = [ref[t, pl.ds(pl.multiple_of(base, 8), 8), :] for t in range(3)]
        up = [ref[t, pl.ds(base - 1, 8), :] for t in range(3)]
        down = [ref[t, pl.ds(base + 1, 8), :] for t in range(3)]
        n, p = nexts(v), prevs(v)
        m = masks(e)
        q = [(0.25 * m[t]) * ((n[t] + p[t]) + (up[t] + down[t]) - 4.0 * v[t]) for t in range(3)]
        gx = [n[t] - p[t] for t in range(3)]
        gy = [down[t] - up[t] for t in range(3)]
        return q, gx, gy

    def gather(e, t):
        base = 8 * e + 8
        return xs[t, pl.ds(pl.multiple_of(8 * e, 8), 8), :] + yp[t, pl.ds(base + 1, 8), :] + ym[t, pl.ds(base - 1, 8), :]

    def linearize(e, carry):
        q, gx, gy = stencil(fields.at[0], e)
        at, to = pl.ds(pl.multiple_of(8 * e + 8, 8), 8), pl.ds(pl.multiple_of(8 * e, 8), 8)
        hx, hy = [], []
        for t in range(3):
            sx, sy = 0.5 * gx[t], 0.5 * gy[t]
            inv = 1.0 / (1.0 + sx * sx + sy * sy)
            a = fields[1, t, at, :] * jnp.sqrt(inv)
            j0, jx, jy = fields[2, t, at, :], fields[3, t, at, :], fields[4, t, at, :]
            tx, ty = sx * inv, sy * inv
            f1x = m10 - sx * m20 - sy * m11
            f1y = m01 - sx * m11 - sy * m02
            f2 = m00 - sx * m10 - sy * m01 - sx * f1x - sy * f1y
            g1x, g1y = f1x + tx * f2, f1y + ty * f2
            jf = j0 - sx * jx - sy * jy
            qa = 0.25 * (a * a)
            coef[0, t, to, :] = qa * (m20 + tx * (f1x + g1x))
            coef[1, t, to, :] = qa * (m11 + ty * f1x + tx * g1y)
            coef[2, t, to, :] = qa * (m02 + ty * (f1y + g1y))
            ha = 0.5 * a
            hx.append(ha * (jx + tx * jf - a * g1x))
            hy.append(ha * (jy + ty * jf - a * g1y))
        scatter(e, q, hx, hy)
        return carry

    def right_side(e, carry):
        m, at = masks(e), pl.ds(pl.multiple_of(8 * e + 8, 8), 8)
        for t in range(3):
            vec_r[t, at, :] = -m[t] * gather(e, t)
        return carry

    def apply_from(ref):
        def body(e, carry):
            q, gx, gy = stencil(ref, e)
            at = pl.ds(pl.multiple_of(8 * e, 8), 8)
            cxx, cxy, cyy = ([coef[j, t, at, :] for t in range(3)] for j in range(3))
            hx = [cxx[t] * gx[t] + cxy[t] * gy[t] for t in range(3)]
            hy = [cxy[t] * gx[t] + cyy[t] * gy[t] for t in range(3)]
            scatter(e, q, hx, hy)
            return carry

        return body

    def image_of_r(e, carry):
        m, at = masks(e), pl.ds(pl.multiple_of(8 * e + 8, 8), 8)
        for t in range(3):
            vec_u[t, at, :] = m[t] * gather(e, t)
        return carry

    def image_of_u(e, acc):
        at = pl.ds(pl.multiple_of(8 * e + 8, 8), 8)
        for t in range(2):
            w = gather(e, t)
            r, u = vec_r[t, at, :], vec_u[t, at, :]
            vec_w[t, pl.ds(pl.multiple_of(8 * e - 8, 8), 8), :] = w
            acc = (acc[0] + r * r, acc[1] + r * u, acc[2] + u * u, acc[3] + u * w)
        return acc

    lax.fori_loop(0, TILES + 2, linearize, 0, unroll=2)
    lax.fori_loop(0, TILES + 2, right_side, 0, unroll=3)
    lax.fori_loop(0, TILES + 2, apply_from(vec_r), 0, unroll=2)
    lax.fori_loop(0, TILES + 2, image_of_r, 0, unroll=3)
    lax.fori_loop(0, TILES + 2, apply_from(vec_u), 0, unroll=2)
    acc = lax.fori_loop(1, TILES + 1, image_of_u, (zero, zero, zero, zero), unroll=4)

    folded = []
    for x in acc:
        x = x + pltpu.roll(x, 64, 1)
        folded.append(x + pltpu.roll(x, 32, 1))
    mixed = jnp.where(lane < 64, jnp.where(lane < 32, folded[0], folded[1]), jnp.where(lane < 96, folded[2], folded[3]))
    mine = jnp.sum(mixed, axis=0, keepdims=True)

    def exchange(stage, mine, slots, count, target):
        part[stage] = mine
        out = [
            pltpu.make_async_remote_copy(
                src_ref=part.at[stage], dst_ref=slots.at[d - 1], send_sem=ar_send.at[stage], recv_sem=ar_recv.at[stage],
                device_id=target(d), device_id_type=MESH,
            )
            for d in range(1, count)
        ]
        for cp in out:
            cp.start()
        pltpu.make_async_copy(slots, slots, ar_recv.at[stage]).wait()
        total = mine
        for d in range(1, count):
            total = total + slots[d - 1]
        return total

    total = exchange(0, mine, sums_row, NR, lambda d: dev(d, 0))
    total = exchange(1, total, sums_col, NC, lambda d: dev(0, d))
    pltpu.make_async_copy(sums_row, sums_row, ar_send.at[0]).wait()
    pltpu.make_async_copy(sums_col, sums_col, ar_send.at[1]).wait()

    lane1 = lax.broadcasted_iota(jnp.int32, (1, 128), 1)

    def quarter(n):
        picked = jnp.where((lane1 >= 32 * n) & (lane1 < 32 * n + 32), total, 0.0)
        return jnp.broadcast_to(jnp.sum(picked, axis=1, keepdims=True), (8, 128))

    rr, ru, uu, uw = (quarter(n) for n in range(4))
    p1, p2, p3 = ru / rr, uu / rr, uw / rr
    step0 = 1.0 / (1.0 + p1)
    keep = p1 * step0
    beta = (p2 - p1 * p1) * (step0 * step0)
    g = keep + beta
    curve = g * g * (1.0 + p1) - 2.0 * g * step0 * (p1 + p2) + step0 * step0 * (p2 + p3)
    step1 = beta / curve
    s_r, s_u = step0 + step1 * g, -step1 * step0
    d_r, d_u, d_w = keep - step1 * g, -step0 - step1 * (g - step0), step1 * step0

    def finish(i, carry):
        at, to = pl.ds(pl.multiple_of(8 * i, 8), 8), pl.ds(pl.multiple_of(8 * i + TOP, 8), 8)
        for t in range(2):
            r, u, w = vec_r[t, to, :], vec_u[t, to, :], vec_w[t, at, :]
            sol_out[at, pl.ds(128 * t, 128)] = s_r * r + s_u * u
            res_out[at, pl.ds(128 * t, 128)] = d_r * r + d_u * u + d_w * w
        return carry

    lax.fori_loop(0, TILES, finish, 0, unroll=4)


def shards(heights, albedo, images, lights):
    padded = pltpu.VMEM((3, ROWS + 32, 128), F32)
    return pl.pallas_call(
        kernel,
        out_shape=[jax.ShapeDtypeStruct((ROWS, COLS), F32)] * 2,
        in_specs=[pl.BlockSpec(memory_space=pltpu.HBM)] * 4,
        out_specs=[pl.BlockSpec(memory_space=pltpu.VMEM)] * 2,
        scratch_shapes=[
            pltpu.VMEM((NF, 3, ROWS + 32, 128), F32),
            pltpu.VMEM((NIMG, ROWS, COLS), F32),
            pltpu.VMEM((2, NIMG), F32),
            pltpu.VMEM((2, ROWS // 2, 128), F32),
            pltpu.VMEM((2, ROWS // 2, 128), F32),
            pltpu.VMEM((2, 2, 8, 128), F32),
            pltpu.VMEM((3, 3, ROWS + 16, 128), F32),
            pltpu.VMEM((3, ROWS + 16, 128), F32),
            padded, padded, padded, padded,
            pltpu.VMEM((2, ROWS, 128), F32),
            pltpu.VMEM((2, 1, 128), F32),
            pltpu.VMEM((NR - 1, 1, 128), F32),
            pltpu.VMEM((NC - 1, 1, 128), F32),
            pltpu.SemaphoreType.DMA((5,)),
            pltpu.SemaphoreType.DMA((NIMG,)),
            pltpu.SemaphoreType.DMA((8,)),
            pltpu.SemaphoreType.DMA((8,)),
            pltpu.SemaphoreType.DMA((2,)),
            pltpu.SemaphoreType.DMA((2,)),
        ],
        compiler_params=pltpu.CompilerParams(collective_id=0, has_side_effects=True, vmem_limit_bytes=40 * 1024 * 1024),
    )(heights, albedo, images, lights.T)


def solution(mesh):
    placed = (P("row", "col"), P("row", "col"), P(None, "row", "col"), P())
    return jax.shard_map(
        shards, mesh=mesh, in_specs=placed, out_specs=(P("row", "col"), P("row", "col")), check_vma=False
    )
```

```python
import jax
import jax.numpy as jnp
from jax import lax
from jax.experimental import pallas as pl
from jax.experimental.pallas import tpu as pltpu
from jax.sharding import PartitionSpec as P

MESH = pl.DeviceIdType.MESH
F32 = jnp.float32
NIMG = 8
NR, NC = 16, 32
ROWS, COLS = 128, 256
TILES = ROWS // 8
NF = 5
TOP = 16
STRIDE = 12


def kernel(
    heights, albedo, images, lights, sol_out, res_out,
    fields, img, light, packs, strips, corners, coef, xs, yp, ym, vec_r, vec_u, vec_w, part, sums_row, sums_col,
    in_sem, img_sem, send_sem, recv_sem, ar_send, ar_recv,
):
    row, col = lax.axis_index("row"), lax.axis_index("col")

    def dev(dr, dc):
        return (lax.rem(row + (dr + NR), NR), lax.rem(col + (dc + NC), NC))

    loads = []
    for f, src in enumerate((heights, albedo)):
        for t in range(2):
            loads.append(
                pltpu.make_async_copy(src.at[:, pl.ds(128 * t, 128)], fields.at[f, t, pl.ds(TOP, ROWS), :], in_sem.at[2 * f + t])
            )
    load_light = pltpu.make_async_copy(lights, light, in_sem.at[4])
    load_img = [pltpu.make_async_copy(images.at[k], img.at[k], img_sem.at[k]) for k in range(NIMG)]
    load_light.start()
    for cp in load_img:
        cp.start()
    for cp in loads:
        cp.start()

    peers = {(a, b) for a in (-1, 0, 1) for b in (-1, 0, 1)} | {(d, 0) for d in range(NR)} | {(0, d) for d in range(NC)}
    peers = sorted({(a % NR, b % NC) for a, b in peers} - {(0, 0)})
    barrier = pltpu.get_barrier_semaphore()
    for p in peers:
        pl.semaphore_signal(barrier, inc=1, device_id=dev(*p), device_id_type=MESH)

    lane = lax.broadcasted_iota(jnp.int32, (8, 128), 1)
    zero = jnp.zeros((8, 128), F32)
    for t in range(3):
        for ref in (fields.at[0], yp, ym, vec_r, vec_u):
            ref[t, pl.ds(0, 8), :] = zero
            ref[t, pl.ds(ROWS + 24, 8), :] = zero

    load_light.wait()
    lx, ly = light[0:1, :], light[1:2, :]
    inv_sq = 1.0 / (1.0 + lx * lx + ly * ly)
    inv_norm = jnp.sqrt(inv_sq)

    def over_images(x):
        return jnp.broadcast_to(jnp.sum(x, axis=1, keepdims=True), (8, 128))

    m00, m10, m01 = over_images(inv_sq), over_images(inv_sq * lx), over_images(inv_sq * ly)
    m20, m11, m02 = over_images(inv_sq * lx * lx), over_images(inv_sq * lx * ly), over_images(inv_sq * ly * ly)
    weights = [
        [jnp.broadcast_to(w[:, k : k + 1], (8, 128)) for w in (inv_norm, inv_norm * lx, inv_norm * ly)] for k in range(NIMG)
    ]

    for cp in load_img:
        cp.wait()

    def image_sums(i, carry):
        at = pl.ds(pl.multiple_of(8 * i, 8), 8)
        to = pl.ds(pl.multiple_of(8 * i + TOP, 8), 8)
        for t in range(2):
            acc = [zero, zero, zero]
            for k in range(NIMG):
                v = img[k, at, pl.ds(128 * t, 128)]
                acc = [acc[j] + weights[k][j] * v for j in range(3)]
            for j in range(3):
                fields[2 + j, t, to, :] = acc[j]
        return carry

    lax.fori_loop(0, TILES, image_sums, 0, unroll=2)
    for cp in loads:
        cp.wait()

    shifts = [(64 * g + STRIDE * f, g, f) for g in range(2) for f in range(NF)]

    def pack(j, carry):
        left, right, first = zero, zero, None
        for s, g, f in shifts:
            at = pl.ds(pl.multiple_of(8 * j + (64 * g + TOP), 8), 8)
            a, b = fields[f, 0, at, :], fields[f, 1, at, :]
            if s:
                a, b = pltpu.roll(a, s, 1), pltpu.roll(b, s, 1)
                left = jnp.where(lane >= s, a, left)
                right = jnp.where(lane >= s - 6, b, right)
            else:
                left, right, first = a, b, b
        to = pl.ds(pl.multiple_of(8 * j, 8), 8)
        packs[0, to, :] = left
        packs[1, to, :] = jnp.where(lane >= 122, first, right)
        return carry

    lax.fori_loop(0, 8, pack, 0, unroll=2)

    pl.semaphore_wait(barrier, len(peers))
    first8, last8 = pl.ds(0, 8), pl.ds(56, 8)
    moves = [
        (packs.at[0, first8, :], corners.at[1, 0], (-1, -1)),
        (packs.at[1, first8, :], corners.at[1, 1], (-1, 1)),
        (packs.at[0, last8, :], corners.at[0, 0], (1, -1)),
        (packs.at[1, last8, :], corners.at[0, 1], (1, 1)),
        (fields.at[:, pl.ds(0, 2), pl.ds(TOP, 8), :], fields.at[:, pl.ds(0, 2), pl.ds(TOP + ROWS, 8), :], (-1, 0)),
        (fields.at[:, pl.ds(0, 2), pl.ds(TOP + ROWS - 8, 8), :], fields.at[:, pl.ds(0, 2), pl.ds(TOP - 8, 8), :], (1, 0)),
        (packs.at[0], strips.at[0], (0, -1)),
        (packs.at[1], strips.at[1], (0, 1)),
    ]
    copies = [
        pltpu.make_async_remote_copy(
            src_ref=src, dst_ref=dst, send_sem=send_sem.at[n], recv_sem=recv_sem.at[n], device_id=dev(*to), device_id_type=MESH
        )
        for n, (src, dst, to) in enumerate(moves)
    ]
    for cp in copies:
        cp.start()
    for cp in copies:
        cp.wait()

    above = jnp.where(row > 0, 1.0, 0.0).astype(F32)
    below = jnp.where(row < NR - 1, 1.0, 0.0).astype(F32)
    before = jnp.where(col > 0, 1.0, 0.0).astype(F32)
    after = jnp.where(col < NC - 1, 1.0, 0.0).astype(F32)
    side_mask = jnp.where(lane < 64, after, before)

    def masks(e):
        m = jnp.where(e == 0, above, jnp.where(e == TILES + 1, below, 1.0))
        return (m, m, m * side_mask)

    in_group = lane & 63
    from_right = in_group < 6
    for f in range(1, NF):
        from_right = from_right | ((in_group >= STRIDE * f) & (in_group < STRIDE * f + 6))

    def side(merged, g, f, at, mask):
        s = 64 * g + STRIDE * f
        v = pltpu.roll(merged, 128 - s, 1) if s else merged
        fields[f, 2, at, :] = v * mask if f < 2 else v

    def unpack(j, carry):
        at = pl.ds(pl.multiple_of(8 * j, 8), 8)
        merged = jnp.where(from_right, strips[0, at, :], strips[1, at, :])
        for s, g, f in shifts:
            side(merged, g, f, pl.ds(pl.multiple_of(8 * j + (64 * g + TOP), 8), 8), side_mask)
        return carry

    lax.fori_loop(0, 8, unpack, 0, unroll=2)
    for b, g, start, ok in ((0, 1, TOP - 8, above), (1, 0, TOP + ROWS, below)):
        merged = jnp.where(from_right, corners[b, 0], corners[b, 1])
        at = pl.ds(start, 8)
        for f in range(NF):
            side(merged, g, f, at, side_mask * ok)
        for f in range(2):
            for t in range(2):
                fields[f, t, at, :] = fields[f, t, at, :] * ok

    is_last, is_first = lane == 127, lane == 0

    def nexts(v):
        r = [pltpu.roll(x, 127, 1) for x in v]
        return [jnp.where(is_last, r[(t + 1) % 3], r[t]) for t in range(3)]

    def prevs(v):
        r = [pltpu.roll(x, 1, 1) for x in v]
        return [jnp.where(is_first, r[(t + 2) % 3], r[t]) for t in range(3)]

    def scatter(e, q, hx, hy):
        n = nexts([q[t] - hx[t] for t in range(3)])
        p = prevs([q[t] + hx[t] for t in range(3)])
        at, to = pl.ds(pl.multiple_of(8 * e, 8), 8), pl.ds(pl.multiple_of(8 * e + 8, 8), 8)
        for t in range(3):
            xs[t, at, :] = n[t] + p[t] - 4.0 * q[t]
            yp[t, to, :] = q[t] - hy[t]
            ym[t, to, :] = q[t] + hy[t]

    def stencil(ref, e):
        base = 8 * e + 8
        v = [ref[t, pl.ds(pl.multiple_of(base, 8), 8), :] for t in range(3)]
        up = [ref[t, pl.ds(base - 1, 8), :] for t in range(3)]
        down = [ref[t, pl.ds(base + 1, 8), :] for t in range(3)]
        n, p = nexts(v), prevs(v)
        m = masks(e)
        q = [(0.25 * m[t]) * ((n[t] + p[t]) + (up[t] + down[t]) - 4.0 * v[t]) for t in range(3)]
        gx = [n[t] - p[t] for t in range(3)]
        gy = [down[t] - up[t] for t in range(3)]
        return q, gx, gy

    def gather(e, t):
        base = 8 * e + 8
        return xs[t, pl.ds(pl.multiple_of(8 * e, 8), 8), :] + yp[t, pl.ds(base + 1, 8), :] + ym[t, pl.ds(base - 1, 8), :]

    def linearize(e, carry):
        q, gx, gy = stencil(fields.at[0], e)
        at, to = pl.ds(pl.multiple_of(8 * e + 8, 8), 8), pl.ds(pl.multiple_of(8 * e, 8), 8)
        hx, hy = [], []
        for t in range(3):
            sx, sy = 0.5 * gx[t], 0.5 * gy[t]
            inv = 1.0 / (1.0 + sx * sx + sy * sy)
            a = fields[1, t, at, :] * jnp.sqrt(inv)
            j0, jx, jy = fields[2, t, at, :], fields[3, t, at, :], fields[4, t, at, :]
            tx, ty = sx * inv, sy * inv
            f1x = m10 - sx * m20 - sy * m11
            f1y = m01 - sx * m11 - sy * m02
            f2 = m00 - sx * m10 - sy * m01 - sx * f1x - sy * f1y
            g1x, g1y = f1x + tx * f2, f1y + ty * f2
            jf = j0 - sx * jx - sy * jy
            qa = 0.25 * (a * a)
            coef[0, t, to, :] = qa * (m20 + tx * (f1x + g1x))
            coef[1, t, to, :] = qa * (m11 + ty * f1x + tx * g1y)
            coef[2, t, to, :] = qa * (m02 + ty * (f1y + g1y))
            ha = 0.5 * a
            hx.append(ha * (jx + tx * jf - a * g1x))
            hy.append(ha * (jy + ty * jf - a * g1y))
        scatter(e, q, hx, hy)
        return carry

    def right_side(e, carry):
        m, at = masks(e), pl.ds(pl.multiple_of(8 * e + 8, 8), 8)
        for t in range(3):
            vec_r[t, at, :] = -m[t] * gather(e, t)
        return carry

    def apply_from(ref):
        def body(e, carry):
            q, gx, gy = stencil(ref, e)
            at = pl.ds(pl.multiple_of(8 * e, 8), 8)
            cxx, cxy, cyy = ([coef[j, t, at, :] for t in range(3)] for j in range(3))
            hx = [cxx[t] * gx[t] + cxy[t] * gy[t] for t in range(3)]
            hy = [cxy[t] * gx[t] + cyy[t] * gy[t] for t in range(3)]
            scatter(e, q, hx, hy)
            return carry

        return body

    def image_of_r(e, carry):
        m, at = masks(e), pl.ds(pl.multiple_of(8 * e + 8, 8), 8)
        for t in range(3):
            vec_u[t, at, :] = m[t] * gather(e, t)
        return carry

    def image_of_u(e, acc):
        at = pl.ds(pl.multiple_of(8 * e + 8, 8), 8)
        for t in range(2):
            w = gather(e, t)
            r, u = vec_r[t, at, :], vec_u[t, at, :]
            vec_w[t, pl.ds(pl.multiple_of(8 * e - 8, 8), 8), :] = w
            acc = (acc[0] + r * r, acc[1] + r * u, acc[2] + u * u, acc[3] + u * w)
        return acc

    lax.fori_loop(0, TILES + 2, linearize, 0, unroll=9)
    lax.fori_loop(0, TILES + 2, right_side, 0, unroll=9)
    lax.fori_loop(0, TILES + 2, apply_from(vec_r), 0, unroll=9)
    lax.fori_loop(0, TILES + 2, image_of_r, 0, unroll=9)
    lax.fori_loop(0, TILES + 2, apply_from(vec_u), 0, unroll=9)
    acc = lax.fori_loop(1, TILES + 1, image_of_u, (zero, zero, zero, zero), unroll=16)

    folded = []
    for x in acc:
        x = x + pltpu.roll(x, 64, 1)
        folded.append(x + pltpu.roll(x, 32, 1))
    mixed = jnp.where(lane < 64, jnp.where(lane < 32, folded[0], folded[1]), jnp.where(lane < 96, folded[2], folded[3]))
    mine = jnp.sum(mixed, axis=0, keepdims=True)

    def exchange(stage, mine, slots, count, target):
        part[stage] = mine
        out = [
            pltpu.make_async_remote_copy(
                src_ref=part.at[stage], dst_ref=slots.at[d - 1], send_sem=ar_send.at[stage], recv_sem=ar_recv.at[stage],
                device_id=target(d), device_id_type=MESH,
            )
            for d in range(1, count)
        ]
        for cp in out:
            cp.start()
        pltpu.make_async_copy(slots, slots, ar_recv.at[stage]).wait()
        total = mine
        for d in range(1, count):
            total = total + slots[d - 1]
        return total

    total = exchange(0, mine, sums_row, NR, lambda d: dev(d, 0))
    total = exchange(1, total, sums_col, NC, lambda d: dev(0, d))
    pltpu.make_async_copy(sums_row, sums_row, ar_send.at[0]).wait()
    pltpu.make_async_copy(sums_col, sums_col, ar_send.at[1]).wait()

    lane1 = lax.broadcasted_iota(jnp.int32, (1, 128), 1)

    def quarter(n):
        picked = jnp.where((lane1 >= 32 * n) & (lane1 < 32 * n + 32), total, 0.0)
        return jnp.broadcast_to(jnp.sum(picked, axis=1, keepdims=True), (8, 128))

    rr, ru, uu, uw = (quarter(n) for n in range(4))
    p1, p2, p3 = ru / rr, uu / rr, uw / rr
    step0 = 1.0 / (1.0 + p1)
    keep = p1 * step0
    beta = (p2 - p1 * p1) * (step0 * step0)
    g = keep + beta
    curve = g * g * (1.0 + p1) - 2.0 * g * step0 * (p1 + p2) + step0 * step0 * (p2 + p3)
    step1 = beta / curve
    s_r, s_u = step0 + step1 * g, -step1 * step0
    d_r, d_u, d_w = keep - step1 * g, -step0 - step1 * (g - step0), step1 * step0

    def finish(i, carry):
        at, to = pl.ds(pl.multiple_of(8 * i, 8), 8), pl.ds(pl.multiple_of(8 * i + TOP, 8), 8)
        for t in range(2):
            r, u, w = vec_r[t, to, :], vec_u[t, to, :], vec_w[t, at, :]
            sol_out[at, pl.ds(128 * t, 128)] = s_r * r + s_u * u
            res_out[at, pl.ds(128 * t, 128)] = d_r * r + d_u * u + d_w * w
        return carry

    lax.fori_loop(0, TILES, finish, 0, unroll=4)


def shards(heights, albedo, images, lights):
    padded = pltpu.VMEM((3, ROWS + 32, 128), F32)
    return pl.pallas_call(
        kernel,
        out_shape=[jax.ShapeDtypeStruct((ROWS, COLS), F32)] * 2,
        in_specs=[pl.BlockSpec(memory_space=pltpu.HBM)] * 4,
        out_specs=[pl.BlockSpec(memory_space=pltpu.VMEM)] * 2,
        scratch_shapes=[
            pltpu.VMEM((NF, 3, ROWS + 32, 128), F32),
            pltpu.VMEM((NIMG, ROWS, COLS), F32),
            pltpu.VMEM((2, NIMG), F32),
            pltpu.VMEM((2, ROWS // 2, 128), F32),
            pltpu.VMEM((2, ROWS // 2, 128), F32),
            pltpu.VMEM((2, 2, 8, 128), F32),
            pltpu.VMEM((3, 3, ROWS + 16, 128), F32),
            pltpu.VMEM((3, ROWS + 16, 128), F32),
            padded, padded, padded, padded,
            pltpu.VMEM((2, ROWS, 128), F32),
            pltpu.VMEM((2, 1, 128), F32),
            pltpu.VMEM((NR - 1, 1, 128), F32),
            pltpu.VMEM((NC - 1, 1, 128), F32),
            pltpu.SemaphoreType.DMA((5,)),
            pltpu.SemaphoreType.DMA((NIMG,)),
            pltpu.SemaphoreType.DMA((8,)),
            pltpu.SemaphoreType.DMA((8,)),
            pltpu.SemaphoreType.DMA((2,)),
            pltpu.SemaphoreType.DMA((2,)),
        ],
        compiler_params=pltpu.CompilerParams(collective_id=0, has_side_effects=True, vmem_limit_bytes=56 * 1024 * 1024),
    )(heights, albedo, images, lights.T)


def solution(mesh):
    placed = (P("row", "col"), P("row", "col"), P(None, "row", "col"), P())
    return jax.shard_map(
        shards, mesh=mesh, in_specs=placed, out_specs=(P("row", "col"), P("row", "col")), check_vma=False
    )
```

```python
import jax
import jax.numpy as jnp
from jax import lax
from jax.experimental import pallas as pl
from jax.experimental.pallas import tpu as pltpu
from jax.sharding import PartitionSpec as P

MESH = pl.DeviceIdType.MESH
F32 = jnp.float32
NIMG = 8
NR, NC = 16, 32
ROWS, COLS = 128, 256
TILES = ROWS // 8
NF = 5
TOP = 16
UN = (4, 8, 7, 4, 9)
STRIDE = 12


def kernel(
    heights, albedo, images, lights, sol_out, res_out,
    fields, img, light, packs, strips, corners, rows_in, coef, xs, yp, ym, vec_r, vec_u, krylov, part, sums_row, sums_col,
    in_sem, img_sem, send_sem, recv_sem, ar_send, ar_recv,
):
    row, col = lax.axis_index("row"), lax.axis_index("col")

    def dev(dr, dc):
        return (lax.rem(row + (dr + NR), NR), lax.rem(col + (dc + NC), NC))

    loads = []
    for f, src in enumerate((heights, albedo)):
        for t in range(2):
            loads.append(
                pltpu.make_async_copy(src.at[:, pl.ds(128 * t, 128)], fields.at[f, t, pl.ds(TOP, ROWS), :], in_sem.at[2 * f + t])
            )
    load_light = pltpu.make_async_copy(lights, light, in_sem.at[4])
    load_img = [pltpu.make_async_copy(images.at[k], img.at[k], img_sem.at[k]) for k in range(NIMG)]
    load_light.start()
    for cp in load_img:
        cp.start()
    for cp in loads:
        cp.start()

    peers = {(a, b) for a in (-1, 0, 1) for b in (-1, 0, 1)} | {(d, 0) for d in range(NR)} | {(0, d) for d in range(NC)}
    peers = sorted({(a % NR, b % NC) for a, b in peers} - {(0, 0)})
    barrier = pltpu.get_barrier_semaphore()
    for p in peers:
        pl.semaphore_signal(barrier, inc=1, device_id=dev(*p), device_id_type=MESH)

    lane = lax.broadcasted_iota(jnp.int32, (8, 128), 1)
    zero = jnp.zeros((8, 128), F32)

    load_light.wait()
    lx, ly = light[0:1, :], light[1:2, :]
    inv_sq = 1.0 / (1.0 + lx * lx + ly * ly)
    inv_norm = jnp.sqrt(inv_sq)

    def over_images(x):
        return jnp.broadcast_to(jnp.sum(x, axis=1, keepdims=True), (8, 128))

    m00, m10, m01 = over_images(inv_sq), over_images(inv_sq * lx), over_images(inv_sq * ly)
    m20, m11, m02 = over_images(inv_sq * lx * lx), over_images(inv_sq * lx * ly), over_images(inv_sq * ly * ly)
    weights = [
        [jnp.broadcast_to(w[:, k : k + 1], (8, 128)) for w in (inv_norm, inv_norm * lx, inv_norm * ly)] for k in range(NIMG)
    ]

    for cp in load_img:
        cp.wait()

    def image_sums(i, carry):
        at = pl.ds(pl.multiple_of(8 * i, 8), 8)
        to = pl.ds(pl.multiple_of(8 * i + TOP, 8), 8)
        for t in range(2):
            acc = [zero, zero, zero]
            for k in range(NIMG):
                v = img[k, at, pl.ds(128 * t, 128)]
                acc = [acc[j] + weights[k][j] * v for j in range(3)]
            for j in range(3):
                fields[2 + j, t, to, :] = acc[j]
        return carry

    lax.fori_loop(0, TILES, image_sums, 0, unroll=2)
    for cp in loads:
        cp.wait()

    def tile(e):
        return pl.ds(pl.multiple_of(8 * e + 8, 8), 8)

    shifts = [(64 * g + STRIDE * f, g, f) for g in range(2) for f in range(NF)]

    def pack(j, carry):
        left, right, first = zero, zero, None
        for s, g, f in shifts:
            a = fields[f, 0, tile(j + (8 * g + 1)), :]
            b = fields[f, 1, tile(j + (8 * (1 - g) + 1)), :]
            if s:
                a, b = pltpu.roll(a, s, 1), pltpu.roll(b, s, 1)
                left = jnp.where(lane >= s, a, left)
                right = jnp.where(lane >= s - 6, b, right)
            else:
                left, right, first = a, b, b
        to = pl.ds(pl.multiple_of(8 * j, 8), 8)
        packs[0, to, :] = left
        packs[1, to, :] = jnp.where(lane >= 122, first, right)
        return carry

    lax.fori_loop(0, 8, pack, 0, unroll=4)

    pl.semaphore_wait(barrier, len(peers))
    first8, last8 = pl.ds(0, 8), pl.ds(56, 8)
    moves = [
        (packs.at[0, first8, :], corners.at[1, 0], (-1, -1)),
        (packs.at[1, first8, :], corners.at[1, 1], (-1, 1)),
        (packs.at[0, last8, :], corners.at[0, 0], (1, -1)),
        (packs.at[1, last8, :], corners.at[0, 1], (1, 1)),
        (fields.at[:, pl.ds(0, 2), pl.ds(TOP, 8), :], rows_in.at[1], (-1, 0)),
        (fields.at[:, pl.ds(0, 2), pl.ds(TOP + ROWS - 8, 8), :], rows_in.at[0], (1, 0)),
        (packs.at[0], strips.at[0], (0, -1)),
        (packs.at[1], strips.at[1], (0, 1)),
    ]
    copies = [
        pltpu.make_async_remote_copy(
            src_ref=src, dst_ref=dst, send_sem=send_sem.at[n], recv_sem=recv_sem.at[n], device_id=dev(*to), device_id_type=MESH
        )
        for n, (src, dst, to) in enumerate(moves)
    ]
    for cp in copies:
        cp.start()

    above = jnp.where(row > 0, 1.0, 0.0).astype(F32)
    below = jnp.where(row < NR - 1, 1.0, 0.0).astype(F32)
    before = jnp.where(col > 0, 1.0, 0.0).astype(F32)
    after = jnp.where(col < NC - 1, 1.0, 0.0).astype(F32)
    side_mask = jnp.where(lane < 64, jnp.where(lane < 32, after, before), 1.0)
    is_last, is_first = lane == 127, lane == 0

    def row_mask(e):
        return jnp.where(e == 0, above, jnp.where(e == TILES + 1, below, 1.0))

    def nexts(v):
        r = [pltpu.roll(x, 127, 1) for x in v]
        return [jnp.where(is_last, r[1], r[0]), r[1]] if len(v) == 2 else r

    def prevs(v):
        r = [pltpu.roll(x, 1, 1) for x in v]
        return [r[0], jnp.where(is_first, r[0], r[1])] if len(v) == 2 else r

    def scatter(k, ts, e, q, hx, hy):
        n = nexts([a - b for a, b in zip(q, hx)])
        p = prevs([a + b for a, b in zip(q, hx)])
        for i, t in enumerate(ts):
            xs[k, t, tile(e), :] = n[i] + p[i] - 4.0 * q[i]
            yp[k, t, tile(e), :] = q[i] - hy[i]
            ym[k, t, tile(e), :] = q[i] + hy[i]

    def stencil(ref, ts, e, mask):
        v = [ref[t, tile(e), :] for t in ts]
        up = [ref[t, pl.ds(8 * e + 7, 8), :] for t in ts]
        down = [ref[t, pl.ds(8 * e + 9, 8), :] for t in ts]
        n, p = nexts(v), prevs(v)
        quarter = 0.25 if mask is None else 0.25 * mask
        q = [quarter * ((a + b) + (c + d) - 4.0 * x) for a, b, c, d, x in zip(n, p, up, down, v)]
        return v, q, [a - b for a, b in zip(n, p)], [a - b for a, b in zip(down, up)]

    def gather(k, t, e):
        return xs[k, t, tile(e), :] + yp[k, t, pl.ds(8 * e + 9, 8), :] + ym[k, t, pl.ds(8 * e + 7, 8), :]

    def mask_of(ts, e, inner):
        if inner:
            return None
        return row_mask(e) * side_mask if ts == (2,) else row_mask(e)

    def linearize(ts, inner, e):
        _, q, gx, gy = stencil(fields.at[0], ts, e, mask_of(ts, e, inner))
        hx, hy = [], []
        for i, t in enumerate(ts):
            sx, sy = 0.5 * gx[i], 0.5 * gy[i]
            inv = 1.0 / (1.0 + sx * sx + sy * sy)
            a = fields[1, t, tile(e), :] * jnp.sqrt(inv)
            j0, jx, jy = (fields[f, t, tile(e), :] for f in (2, 3, 4))
            tx, ty = sx * inv, sy * inv
            f1x = m10 - sx * m20 - sy * m11
            f1y = m01 - sx * m11 - sy * m02
            f2 = m00 - sx * m10 - sy * m01 - sx * f1x - sy * f1y
            g1x, g1y = f1x + tx * f2, f1y + ty * f2
            jf = j0 - sx * jx - sy * jy
            qa = 0.25 * (a * a)
            coef[0, t, tile(e), :] = qa * (m20 + tx * (f1x + g1x))
            coef[1, t, tile(e), :] = qa * (m11 + ty * f1x + tx * g1y)
            coef[2, t, tile(e), :] = qa * (m02 + ty * (f1y + g1y))
            ha = 0.5 * a
            hx.append(ha * (jx + tx * jf - a * g1x))
            hy.append(ha * (jy + ty * jf - a * g1y))
        scatter(0, ts, e, q, hx, hy)

    def right_side(ts, inner, e):
        m = mask_of(ts, e, inner)
        for t in ts:
            v = gather(0, t, e)
            vec_r[t, tile(e), :] = -v if m is None else -m * v

    def image_of_r(ts, inner, e):
        m = mask_of(ts, e, inner)
        for t in ts:
            v = gather(1, t, e)
            vec_u[t, tile(e), :] = v if m is None else m * v

    def weighted(ref, ts, e, mask):
        v, q, gx, gy = stencil(ref, ts, e, mask)
        cxx, cxy, cyy = ([coef[j, t, tile(e), :] for t in ts] for j in range(3))
        hx = [a * x + b * y for a, b, x, y in zip(cxx, cxy, gx, gy)]
        hy = [a * x + b * y for a, b, x, y in zip(cxy, cyy, gx, gy)]
        return v, q, gx, gy, hx, hy

    def apply_r(ts, inner, e):
        _, q, _, _, hx, hy = weighted(vec_r, ts, e, mask_of(ts, e, inner))
        scatter(1, ts, e, q, hx, hy)

    counts = {0: lane >= 8, 1: lane < 120, 2: ((lane >= 64) & (lane < 72)) | (lane >= 120)}

    def apply_u(ts, inner, e, acc, own=None):
        u, q, gx, gy, hx, hy = weighted(vec_u, ts, e, mask_of(ts, e, inner))
        scatter(2, ts, e, q, hx, hy)
        for i, t in enumerate(ts):
            ok = counts[t] if own is None else counts[t] & own
            r = vec_r[t, tile(e), :]
            terms = (r * r, r * u[i], u[i] * u[i], gx[i] * hx[i] + gy[i] * hy[i] + 4.0 * (q[i] * q[i]))
            acc = tuple(a + jnp.where(ok, x, 0.0) for a, x in zip(acc, terms))
        return acc

    def over(lo, hi, body, unroll):
        def step(e, carry):
            body(e)
            return carry

        lax.fori_loop(lo, hi, step, 0, unroll=unroll)

    main, edge = (0, 1), (2,)

    def own_edge(e):
        for f in range(NF):
            fields[f, 2, tile(e), :] = jnp.where(lane < 96, pltpu.roll(fields[f, 0, tile(e), :], 64, 1), fields[f, 1, tile(e), :])

    over(1, TILES + 1, own_edge, UN[0])
    over(1, TILES + 1, lambda e: linearize(main, True, e), UN[1])
    over(1, TILES + 1, lambda e: right_side(main, True, e), UN[1])
    over(1, TILES + 1, lambda e: apply_r(main, True, e), UN[1])
    over(1, TILES + 1, lambda e: image_of_r(main, True, e), UN[1])
    acc = lax.fori_loop(2, TILES, lambda e, acc: apply_u(main, True, e, acc), (zero, zero, zero, zero), unroll=UN[2])

    for cp in copies:
        cp.wait_recv()

    in_group = lane & 63
    from_right = in_group < 6
    for f in range(1, NF):
        from_right = from_right | ((in_group >= STRIDE * f) & (in_group < STRIDE * f + 6))

    def outer(merged, g, f):
        s = 64 * g + STRIDE * f
        return pltpu.roll(merged, 128 - s, 1) if s else merged

    def unpack(j):
        at = pl.ds(pl.multiple_of(8 * j, 8), 8)
        merged = jnp.where(from_right, strips[0, at, :], strips[1, at, :])
        for s, g, f in shifts:
            to = tile(j + (8 * g + 1))
            v = outer(merged, g, f)
            fields[f, 2, to, :] = jnp.where(lane < 64, v * side_mask if f < 2 else v, fields[f, 2, to, :])

    over(0, 8, unpack, UN[3])
    for b, g, e, ok in ((0, 1, 0, above), (1, 0, TILES + 1, below)):
        merged = jnp.where(from_right, corners[b, 0], corners[b, 1])
        for f in range(NF):
            v0, v1 = rows_in[b, f, 0], rows_in[b, f, 1]
            v = jnp.where(lane < 64, outer(merged, g, f), jnp.where(lane < 96, pltpu.roll(v0, 64, 1), v1))
            fields[f, 0, tile(e), :] = v0 * ok if f < 2 else v0
            fields[f, 1, tile(e), :] = v1 * ok if f < 2 else v1
            fields[f, 2, tile(e), :] = v * (side_mask * ok) if f < 2 else v

    def both(body):
        over(0, TILES + 2, lambda e: body(edge, False, e), UN[4])
        over(0, 4, lambda i: body(main, False, i + (TILES - 2) * (i // 2)), 4)

    both(linearize)
    both(right_side)
    both(apply_r)
    both(image_of_r)

    def inside(e):
        return (jnp.zeros((8, 128), jnp.int32) + e >= 1) & (jnp.zeros((8, 128), jnp.int32) + e <= TILES)

    acc = lax.fori_loop(0, TILES + 2, lambda e, acc: apply_u(edge, False, e, acc, inside(e)), acc, unroll=UN[4])

    def last_rows(i, acc):
        e = i + (TILES - 2) * (i // 2)
        return apply_u(main, False, e, acc, inside(e))

    acc = lax.fori_loop(0, 4, last_rows, acc, unroll=4)

    folded = []
    for x in acc:
        x = x + pltpu.roll(x, 64, 1)
        folded.append(x + pltpu.roll(x, 32, 1))
    mixed = jnp.where(lane < 64, jnp.where(lane < 32, folded[0], folded[1]), jnp.where(lane < 96, folded[2], folded[3]))
    mine = jnp.sum(mixed, axis=0, keepdims=True)

    def exchange(stage, mine, slots, count, target, meanwhile):
        part[stage] = mine
        out = [
            pltpu.make_async_remote_copy(
                src_ref=part.at[stage], dst_ref=slots.at[d - 1], send_sem=ar_send.at[stage], recv_sem=ar_recv.at[stage],
                device_id=target(d), device_id_type=MESH,
            )
            for d in range(1, count)
        ]
        for cp in out:
            cp.start()
        meanwhile()
        pltpu.make_async_copy(slots, slots, ar_recv.at[stage]).wait()
        total = mine
        for d in range(1, count):
            total = total + slots[d - 1]
        return total

    def joined(ref, e):
        side = ref[2, tile(e), :] if not isinstance(ref, int) else gather(ref, 2, e)
        inner = [ref[t, tile(e), :] if not isinstance(ref, int) else gather(ref, t, e) for t in main]
        return jnp.where(lane < 8, pltpu.roll(side, 64, 1), inner[0]), jnp.where(lane >= 120, side, inner[1])

    def merge(e):
        at = pl.ds(pl.multiple_of(8 * e - 8, 8), 8)
        for n, ref in enumerate((vec_r, vec_u, 2)):
            for t, v in enumerate(joined(ref, e)):
                krylov[n, at, pl.ds(128 * t, 128)] = v

    total = exchange(0, mine, sums_row, NR, lambda d: dev(d, 0), lambda: over(1, TILES + 1, merge, 4))

    def settle():
        for cp in copies:
            cp.wait_send()
        pltpu.make_async_copy(sums_row, sums_row, ar_send.at[0]).wait()

    total = exchange(1, total, sums_col, NC, lambda d: dev(0, d), settle)

    lane1 = lax.broadcasted_iota(jnp.int32, (1, 128), 1)

    def quarter(n):
        picked = jnp.where((lane1 >= 32 * n) & (lane1 < 32 * n + 32), total, 0.0)
        return jnp.broadcast_to(jnp.sum(picked, axis=1, keepdims=True), (8, 128))

    rr, ru, uu, uw = (quarter(n) for n in range(4))
    p1, p2, p3 = ru / rr, uu / rr, uw / rr
    step0 = 1.0 / (1.0 + p1)
    keep = p1 * step0
    beta = (p2 - p1 * p1) * (step0 * step0)
    g = keep + beta
    curve = g * g * (1.0 + p1) - 2.0 * g * step0 * (p1 + p2) + step0 * step0 * (p2 + p3)
    step1 = beta / curve
    s_r, s_u = step0 + step1 * g, -step1 * step0
    d_r, d_u, d_w = keep - step1 * g, -step0 - step1 * (g - step0), step1 * step0

    def finish(i):
        at = pl.ds(pl.multiple_of(8 * i, 8), 8)
        for t in range(2):
            lanes = pl.ds(128 * t, 128)
            r, u, w = (krylov[n, at, lanes] for n in range(3))
            sol_out[at, lanes] = s_r * r + s_u * u
            res_out[at, lanes] = d_r * r + d_u * u + d_w * w

    over(0, TILES, finish, 4)
    pltpu.make_async_copy(sums_col, sums_col, ar_send.at[1]).wait()


def shards(heights, albedo, images, lights):
    padded = pltpu.VMEM((3, ROWS + 32, 128), F32)
    stacked = pltpu.VMEM((3, 3, ROWS + 32, 128), F32)
    return pl.pallas_call(
        kernel,
        out_shape=[jax.ShapeDtypeStruct((ROWS, COLS), F32)] * 2,
        in_specs=[pl.BlockSpec(memory_space=pltpu.HBM)] * 4,
        out_specs=[pl.BlockSpec(memory_space=pltpu.VMEM)] * 2,
        scratch_shapes=[
            pltpu.VMEM((NF, 3, ROWS + 32, 128), F32),
            pltpu.VMEM((NIMG, ROWS, COLS), F32),
            pltpu.VMEM((2, NIMG), F32),
            pltpu.VMEM((2, ROWS // 2, 128), F32),
            pltpu.VMEM((2, ROWS // 2, 128), F32),
            pltpu.VMEM((2, 2, 8, 128), F32),
            pltpu.VMEM((2, NF, 2, 8, 128), F32),
            stacked,
            stacked, stacked, stacked,
            padded, padded,
            pltpu.VMEM((3, ROWS, COLS), F32),
            pltpu.VMEM((2, 1, 128), F32),
            pltpu.VMEM((NR - 1, 1, 128), F32),
            pltpu.VMEM((NC - 1, 1, 128), F32),
            pltpu.SemaphoreType.DMA((5,)),
            pltpu.SemaphoreType.DMA((NIMG,)),
            pltpu.SemaphoreType.DMA((8,)),
            pltpu.SemaphoreType.DMA((8,)),
            pltpu.SemaphoreType.DMA((2,)),
            pltpu.SemaphoreType.DMA((2,)),
        ],
        compiler_params=pltpu.CompilerParams(collective_id=0, has_side_effects=True, vmem_limit_bytes=40 * 1024 * 1024),
    )(*(pltpu.with_memory_space_constraint(x, pltpu.HBM) for x in (heights, albedo, images, lights.T)))


def solution(mesh):
    placed = (P("row", "col"), P("row", "col"), P(None, "row", "col"), P())
    return jax.shard_map(
        shards, mesh=mesh, in_specs=placed, out_specs=(P("row", "col"), P("row", "col")), check_vma=False
    )
```

```python
import jax
import jax.numpy as jnp
from jax import lax
from jax.experimental import pallas as pl
from jax.experimental.pallas import tpu as pltpu
from jax.sharding import PartitionSpec as P

MESH = pl.DeviceIdType.MESH
F32 = jnp.float32
NIMG = 8
NR, NC = 16, 32
ROWS, COLS = 128, 256
TILES = ROWS // 8
HALF = TILES // 2 + 1
NF = 5
TOP = 16
UN = (4, 8, 7, 4, 9)
STRIDE = 12


def around(d, count):
    return min(d % count, -d % count)


def kernel(
    heights, albedo, images, lights, out,
    fields, img, light, packs, strips, corners, rows_in, coef, xs, yp, ym, vec_r, vec_u, krylov, part, sums_row, sums_col,
    in_sem, img_sem, send_sem, recv_sem, ar_send, ar_recv,
):
    row, col = lax.axis_index("row"), lax.axis_index("col")

    def dev(dr, dc):
        return (lax.rem(row + (dr + NR), NR), lax.rem(col + (dc + NC), NC))

    peers = {(a, b) for a in (-1, 0, 1) for b in (-1, 0, 1)} | {(d, 0) for d in range(NR)} | {(0, d) for d in range(NC)}
    peers = {(a % NR, b % NC) for a, b in peers} - {(0, 0)}
    peers = sorted(peers, key=lambda p: (p[0] == 0, -around(p[0], NR), -around(p[1], NC), p))
    barrier = pltpu.get_barrier_semaphore()
    for p in peers:
        pl.semaphore_signal(barrier, inc=1, device_id=dev(*p), device_id_type=MESH)

    loads = []
    for f, src in enumerate((heights, albedo)):
        for t in range(2):
            loads.append(
                pltpu.make_async_copy(src.at[:, pl.ds(128 * t, 128)], fields.at[f, t, pl.ds(TOP, ROWS), :], in_sem.at[2 * f + t])
            )
    load_light = pltpu.make_async_copy(lights, light, in_sem.at[4])
    load_img = [pltpu.make_async_copy(images.at[k], img.at[k], img_sem.at[k]) for k in range(NIMG)]
    load_light.start()
    for cp in load_img:
        cp.start()
    for cp in loads:
        cp.start()

    lane = lax.broadcasted_iota(jnp.int32, (8, 128), 1)
    zero = jnp.zeros((8, 128), F32)

    load_light.wait()
    lx, ly = light[0:1, :], light[1:2, :]
    inv_sq = 1.0 / (1.0 + lx * lx + ly * ly)
    inv_norm = jnp.sqrt(inv_sq)

    def over_images(x):
        return jnp.broadcast_to(jnp.sum(x, axis=1, keepdims=True), (8, 128))

    m00, m10, m01 = over_images(inv_sq), over_images(inv_sq * lx), over_images(inv_sq * ly)
    m20, m11, m02 = over_images(inv_sq * lx * lx), over_images(inv_sq * lx * ly), over_images(inv_sq * ly * ly)
    weights = [
        [jnp.broadcast_to(w[:, k : k + 1], (8, 128)) for w in (inv_norm, inv_norm * lx, inv_norm * ly)] for k in range(NIMG)
    ]

    for cp in load_img:
        cp.wait()

    def image_sums(i, carry):
        at = pl.ds(pl.multiple_of(8 * i, 8), 8)
        to = pl.ds(pl.multiple_of(8 * i + TOP, 8), 8)
        for t in range(2):
            acc = [zero, zero, zero]
            for k in range(NIMG):
                v = img[k, at, pl.ds(128 * t, 128)]
                acc = [acc[j] + weights[k][j] * v for j in range(3)]
            for j in range(3):
                fields[2 + j, t, to, :] = acc[j]
        return carry

    lax.fori_loop(0, TILES, image_sums, 0, unroll=2)
    for cp in loads:
        cp.wait()

    def tile(e):
        return pl.ds(pl.multiple_of(8 * e + 8, 8), 8)

    shifts = [(64 * g + STRIDE * f, g, f) for g in range(2) for f in range(NF)]

    def pack(j, carry):
        left, right, first = zero, zero, None
        for s, g, f in shifts:
            a = fields[f, 0, tile(j + (8 * g + 1)), :]
            b = fields[f, 1, tile(j + (8 * (1 - g) + 1)), :]
            if s:
                a, b = pltpu.roll(a, s, 1), pltpu.roll(b, s, 1)
                left = jnp.where(lane >= s, a, left)
                right = jnp.where(lane >= s - 6, b, right)
            else:
                left, right, first = a, b, b
        to = pl.ds(pl.multiple_of(8 * j, 8), 8)
        packs[0, to, :] = left
        packs[1, to, :] = jnp.where(lane >= 122, first, right)
        return carry

    lax.fori_loop(0, 8, pack, 0, unroll=4)

    pl.semaphore_wait(barrier, len(peers))
    first8, last8 = pl.ds(0, 8), pl.ds(56, 8)
    moves = [
        (packs.at[0, first8, :], corners.at[1, 0], (-1, -1)),
        (packs.at[1, first8, :], corners.at[1, 1], (-1, 1)),
        (packs.at[0, last8, :], corners.at[0, 0], (1, -1)),
        (packs.at[1, last8, :], corners.at[0, 1], (1, 1)),
        (fields.at[:, pl.ds(0, 2), pl.ds(TOP, 8), :], rows_in.at[1], (-1, 0)),
        (fields.at[:, pl.ds(0, 2), pl.ds(TOP + ROWS - 8, 8), :], rows_in.at[0], (1, 0)),
        (packs.at[0], strips.at[0], (0, -1)),
        (packs.at[1], strips.at[1], (0, 1)),
    ]
    copies = [
        pltpu.make_async_remote_copy(
            src_ref=src, dst_ref=dst, send_sem=send_sem.at[n], recv_sem=recv_sem.at[n], device_id=dev(*to), device_id_type=MESH
        )
        for n, (src, dst, to) in enumerate(moves)
    ]
    for cp in copies:
        cp.start()

    above = jnp.where(row > 0, 1.0, 0.0).astype(F32)
    below = jnp.where(row < NR - 1, 1.0, 0.0).astype(F32)
    before = jnp.where(col > 0, 1.0, 0.0).astype(F32)
    after = jnp.where(col < NC - 1, 1.0, 0.0).astype(F32)
    side_mask = jnp.where(lane < 64, jnp.where(lane < 32, after, before), 1.0)
    is_last, is_first = lane == 127, lane == 0

    def row_mask(e):
        return jnp.where(e == 0, above, jnp.where(e == TILES + 1, below, 1.0))

    def nexts(v):
        r = [pltpu.roll(x, 127, 1) for x in v]
        return [jnp.where(is_last, r[1], r[0]), r[1]] if len(v) == 2 else r

    def prevs(v):
        r = [pltpu.roll(x, 1, 1) for x in v]
        return [r[0], jnp.where(is_first, r[0], r[1])] if len(v) == 2 else r

    def scatter(k, ts, e, q, hx, hy):
        n = nexts([a - b for a, b in zip(q, hx)])
        p = prevs([a + b for a, b in zip(q, hx)])
        for i, t in enumerate(ts):
            xs[k, t, tile(e), :] = n[i] + p[i] - 4.0 * q[i]
            yp[k, t, tile(e), :] = q[i] - hy[i]
            ym[k, t, tile(e), :] = q[i] + hy[i]

    def stencil(ref, ts, e, mask):
        v = [ref[t, tile(e), :] for t in ts]
        up = [ref[t, pl.ds(8 * e + 7, 8), :] for t in ts]
        down = [ref[t, pl.ds(8 * e + 9, 8), :] for t in ts]
        n, p = nexts(v), prevs(v)
        quarter = 0.25 if mask is None else 0.25 * mask
        q = [quarter * ((a + b) + (c + d) - 4.0 * x) for a, b, c, d, x in zip(n, p, up, down, v)]
        return v, q, [a - b for a, b in zip(n, p)], [a - b for a, b in zip(down, up)]

    def gather(k, t, e):
        return xs[k, t, tile(e), :] + yp[k, t, pl.ds(8 * e + 9, 8), :] + ym[k, t, pl.ds(8 * e + 7, 8), :]

    def mask_of(ts, e, inner):
        if inner:
            return None
        return row_mask(e) * side_mask if ts == (2,) else row_mask(e)

    def linearize(ts, inner, e):
        _, q, gx, gy = stencil(fields.at[0], ts, e, mask_of(ts, e, inner))
        hx, hy = [], []
        for i, t in enumerate(ts):
            sx, sy = 0.5 * gx[i], 0.5 * gy[i]
            inv = 1.0 / (1.0 + sx * sx + sy * sy)
            a = fields[1, t, tile(e), :] * jnp.sqrt(inv)
            j0, jx, jy = (fields[f, t, tile(e), :] for f in (2, 3, 4))
            tx, ty = sx * inv, sy * inv
            f1x = m10 - sx * m20 - sy * m11
            f1y = m01 - sx * m11 - sy * m02
            f2 = m00 - sx * m10 - sy * m01 - sx * f1x - sy * f1y
            g1x, g1y = f1x + tx * f2, f1y + ty * f2
            jf = j0 - sx * jx - sy * jy
            qa = 0.25 * (a * a)
            coef[0, t, tile(e), :] = qa * (m20 + tx * (f1x + g1x))
            coef[1, t, tile(e), :] = qa * (m11 + ty * f1x + tx * g1y)
            coef[2, t, tile(e), :] = qa * (m02 + ty * (f1y + g1y))
            ha = 0.5 * a
            hx.append(ha * (jx + tx * jf - a * g1x))
            hy.append(ha * (jy + ty * jf - a * g1y))
        scatter(0, ts, e, q, hx, hy)

    def right_side(ts, inner, e):
        m = mask_of(ts, e, inner)
        for t in ts:
            v = gather(0, t, e)
            vec_r[t, tile(e), :] = -v if m is None else -m * v

    def image_of_r(ts, inner, e):
        m = mask_of(ts, e, inner)
        for t in ts:
            v = gather(1, t, e)
            vec_u[t, tile(e), :] = v if m is None else m * v

    def weighted(ref, ts, e, mask):
        v, q, gx, gy = stencil(ref, ts, e, mask)
        cxx, cxy, cyy = ([coef[j, t, tile(e), :] for t in ts] for j in range(3))
        hx = [a * x + b * y for a, b, x, y in zip(cxx, cxy, gx, gy)]
        hy = [a * x + b * y for a, b, x, y in zip(cxy, cyy, gx, gy)]
        return v, q, gx, gy, hx, hy

    def apply_r(ts, inner, e):
        _, q, _, _, hx, hy = weighted(vec_r, ts, e, mask_of(ts, e, inner))
        scatter(1, ts, e, q, hx, hy)

    counts = {0: lane >= 8, 1: lane < 120, 2: ((lane >= 64) & (lane < 72)) | (lane >= 120)}

    def apply_u(ts, inner, e, acc, own=None):
        u, q, gx, gy, hx, hy = weighted(vec_u, ts, e, mask_of(ts, e, inner))
        scatter(2, ts, e, q, hx, hy)
        for i, t in enumerate(ts):
            ok = counts[t] if own is None else counts[t] & own
            r = vec_r[t, tile(e), :]
            terms = (r * r, r * u[i], u[i] * u[i], gx[i] * hx[i] + gy[i] * hy[i] + 4.0 * (q[i] * q[i]))
            acc = tuple(a + jnp.where(ok, x, 0.0) for a, x in zip(acc, terms))
        return acc

    def over(lo, hi, body, unroll):
        def step(e, carry):
            body(e)
            return carry

        lax.fori_loop(lo, hi, step, 0, unroll=unroll)

    main, edge = (0, 1), (2,)

    def own_edge(e):
        for f in range(NF):
            fields[f, 2, tile(e), :] = jnp.where(lane < 96, pltpu.roll(fields[f, 0, tile(e), :], 64, 1), fields[f, 1, tile(e), :])

    over(1, TILES + 1, own_edge, UN[0])
    over(1, TILES + 1, lambda e: linearize(main, True, e), UN[1])
    over(1, TILES + 1, lambda e: right_side(main, True, e), UN[1])
    over(1, TILES + 1, lambda e: apply_r(main, True, e), UN[1])
    over(1, TILES + 1, lambda e: image_of_r(main, True, e), UN[1])
    acc = lax.fori_loop(2, TILES, lambda e, acc: apply_u(main, True, e, acc), (zero, zero, zero, zero), unroll=UN[2])

    for cp in copies:
        cp.wait_recv()

    in_group = lane & 63
    from_right = in_group < 6
    for f in range(1, NF):
        from_right = from_right | ((in_group >= STRIDE * f) & (in_group < STRIDE * f + 6))

    def outer(merged, g, f):
        s = 64 * g + STRIDE * f
        return pltpu.roll(merged, 128 - s, 1) if s else merged

    def unpack(j):
        at = pl.ds(pl.multiple_of(8 * j, 8), 8)
        merged = jnp.where(from_right, strips[0, at, :], strips[1, at, :])
        for s, g, f in shifts:
            to = tile(j + (8 * g + 1))
            v = outer(merged, g, f)
            fields[f, 2, to, :] = jnp.where(lane < 64, v * side_mask if f < 2 else v, fields[f, 2, to, :])

    over(0, 8, unpack, UN[3])
    for b, g, e, ok in ((0, 1, 0, above), (1, 0, TILES + 1, below)):
        merged = jnp.where(from_right, corners[b, 0], corners[b, 1])
        for f in range(NF):
            v0, v1 = rows_in[b, f, 0], rows_in[b, f, 1]
            v = jnp.where(lane < 64, outer(merged, g, f), jnp.where(lane < 96, pltpu.roll(v0, 64, 1), v1))
            fields[f, 0, tile(e), :] = v0 * ok if f < 2 else v0
            fields[f, 1, tile(e), :] = v1 * ok if f < 2 else v1
            fields[f, 2, tile(e), :] = v * (side_mask * ok) if f < 2 else v

    def both(body):
        def step(i, carry):
            for j in range(2):
                body(main, False, TILES * i + j)
            for j in range(HALF):
                body(edge, False, HALF * i + j)
            return carry

        lax.fori_loop(0, 2, step, 0, unroll=2)

    both(linearize)
    both(right_side)
    both(apply_r)
    both(image_of_r)

    def inside(e):
        return (jnp.zeros((8, 128), jnp.int32) + e >= 1) & (jnp.zeros((8, 128), jnp.int32) + e <= TILES)

    def last(i, acc):
        for j in range(2):
            acc = apply_u(main, False, TILES * i + j, acc, inside(TILES * i + j))
        for j in range(HALF):
            acc = apply_u(edge, False, HALF * i + j, acc, inside(HALF * i + j))
        return acc

    acc = lax.fori_loop(0, 2, last, acc, unroll=2)

    folded = []
    for x in acc:
        x = x + pltpu.roll(x, 64, 1)
        folded.append(x + pltpu.roll(x, 32, 1))
    mixed = jnp.where(lane < 64, jnp.where(lane < 32, folded[0], folded[1]), jnp.where(lane < 96, folded[2], folded[3]))
    mine = jnp.sum(mixed, axis=0, keepdims=True)

    def exchange(stage, mine, slots, count, target, far, meanwhile):
        part[stage] = mine
        out = [
            pltpu.make_async_remote_copy(
                src_ref=part.at[stage], dst_ref=slots.at[d - 1], send_sem=ar_send.at[stage], recv_sem=ar_recv.at[stage],
                device_id=target(d), device_id_type=MESH,
            )
            for d in sorted(range(1, count), key=lambda d: -far(d))
        ]
        for cp in out:
            cp.start()
        meanwhile()
        pltpu.make_async_copy(slots, slots, ar_recv.at[stage]).wait()
        total = mine
        for d in range(1, count):
            total = total + slots[d - 1]
        return total

    def joined(ref, e):
        side = ref[2, tile(e), :] if not isinstance(ref, int) else gather(ref, 2, e)
        inner = [ref[t, tile(e), :] if not isinstance(ref, int) else gather(ref, t, e) for t in main]
        return jnp.where(lane < 8, pltpu.roll(side, 64, 1), inner[0]), jnp.where(lane >= 120, side, inner[1])

    def merge(e):
        at = pl.ds(pl.multiple_of(8 * e - 8, 8), 8)
        for n, ref in enumerate((vec_r, vec_u, 2)):
            for t, v in enumerate(joined(ref, e)):
                krylov[n, at, pl.ds(128 * t, 128)] = v

    total = exchange(0, mine, sums_row, NR, lambda d: dev(d, 0), lambda d: around(d // 4, 4) + around(d, 4), lambda: over(1, TILES + 1, merge, 4))

    def settle():
        for cp in copies:
            cp.wait_send()
        pltpu.make_async_copy(sums_row, sums_row, ar_send.at[0]).wait()

    total = exchange(1, total, sums_col, NC, lambda d: dev(0, d), lambda d: around(d, NC), settle)

    lane1 = lax.broadcasted_iota(jnp.int32, (1, 128), 1)

    def quarter(n):
        picked = jnp.where((lane1 >= 32 * n) & (lane1 < 32 * n + 32), total, 0.0)
        return jnp.broadcast_to(jnp.sum(picked, axis=1, keepdims=True), (8, 128))

    rr, ru, uu, uw = (quarter(n) for n in range(4))
    p1, p2, p3 = ru / rr, uu / rr, uw / rr
    step0 = 1.0 / (1.0 + p1)
    keep = p1 * step0
    beta = (p2 - p1 * p1) * (step0 * step0)
    g = keep + beta
    curve = g * g * (1.0 + p1) - 2.0 * g * step0 * (p1 + p2) + step0 * step0 * (p2 + p3)
    step1 = beta / curve
    s_r, s_u = step0 + step1 * g, -step1 * step0
    d_r, d_u, d_w = keep - step1 * g, -step0 - step1 * (g - step0), step1 * step0

    def finish(i):
        at = pl.ds(pl.multiple_of(8 * i, 8), 8)
        for t in range(2):
            lanes = pl.ds(128 * t, 128)
            r, u, w = (krylov[n, at, lanes] for n in range(3))
            out[0, at, lanes] = s_r * r + s_u * u
            out[1, at, lanes] = d_r * r + d_u * u + d_w * w

    over(0, TILES, finish, 4)
    pltpu.make_async_copy(sums_col, sums_col, ar_send.at[1]).wait()


def shards(heights, albedo, images, lights):
    padded = pltpu.VMEM((3, ROWS + 32, 128), F32)
    stacked = pltpu.VMEM((3, 3, ROWS + 32, 128), F32)
    out = pl.pallas_call(
        kernel,
        out_shape=jax.ShapeDtypeStruct((2, ROWS, COLS), F32),
        in_specs=[pl.BlockSpec(memory_space=pltpu.HBM)] * 4,
        out_specs=pl.BlockSpec(memory_space=pltpu.VMEM),
        scratch_shapes=[
            pltpu.VMEM((NF, 3, ROWS + 32, 128), F32),
            pltpu.VMEM((NIMG, ROWS, COLS), F32),
            pltpu.VMEM((2, NIMG), F32),
            pltpu.VMEM((2, ROWS // 2, 128), F32),
            pltpu.VMEM((2, ROWS // 2, 128), F32),
            pltpu.VMEM((2, 2, 8, 128), F32),
            pltpu.VMEM((2, NF, 2, 8, 128), F32),
            stacked,
            stacked, stacked, stacked,
            padded, padded,
            pltpu.VMEM((3, ROWS, COLS), F32),
            pltpu.VMEM((2, 1, 128), F32),
            pltpu.VMEM((NR - 1, 1, 128), F32),
            pltpu.VMEM((NC - 1, 1, 128), F32),
            pltpu.SemaphoreType.DMA((5,)),
            pltpu.SemaphoreType.DMA((NIMG,)),
            pltpu.SemaphoreType.DMA((8,)),
            pltpu.SemaphoreType.DMA((8,)),
            pltpu.SemaphoreType.DMA((2,)),
            pltpu.SemaphoreType.DMA((2,)),
        ],
        compiler_params=pltpu.CompilerParams(collective_id=0, has_side_effects=True, vmem_limit_bytes=40 * 1024 * 1024),
    )(*(pltpu.with_memory_space_constraint(x, pltpu.HBM) for x in (heights, albedo, images, lights.T)))
    return out[0], out[1]


def solution(mesh):
    placed = (P("row", "col"), P("row", "col"), P(None, "row", "col"), P())
    return jax.shard_map(
        shards, mesh=mesh, in_specs=placed, out_specs=(P("row", "col"), P("row", "col")), check_vma=False
    )
```

```python
import jax
import jax.numpy as jnp
from jax import lax
from jax.experimental import pallas as pl
from jax.experimental.pallas import tpu as pltpu
from jax.sharding import PartitionSpec as P

MESH = pl.DeviceIdType.MESH
F32 = jnp.float32
NIMG = 8
NR, NC = 16, 32
ROWS, COLS = 128, 256
TILES = ROWS // 8
HALF = TILES // 2 + 1
NF = 5
TOP = 16
UN = (4, 8, 7, 8, 9)
STRIDE = 12


def around(d, count):
    return min(d % count, -d % count)


def kernel(
    heights, albedo, images, lights, out,
    fields, img, light, packs, strips, corners, rows_in, coef, xs, yp, ym, vec_r, vec_u, krylov, part, sums_row, sums_col, sums_all,
    in_sem, img_sem, send_sem, recv_sem, ar_send, ar_recv,
):
    row, col = lax.axis_index("row"), lax.axis_index("col")

    def dev(dr, dc):
        return (lax.rem(row + (dr + NR), NR), lax.rem(col + (dc + NC), NC))

    peers = {(a, b) for a in (-1, 0, 1) for b in (-1, 0, 1)} | {(d, 0) for d in range(NR)} | {(0, d) for d in range(NC)}
    peers = {(a % NR, b % NC) for a, b in peers} - {(0, 0)}
    peers = sorted(peers, key=lambda p: (p[0] == 0, -around(p[0], NR), -around(p[1], NC), p))
    barrier = pltpu.get_barrier_semaphore()
    for p in peers:
        pl.semaphore_signal(barrier, inc=1, device_id=dev(*p), device_id_type=MESH)

    first = (row == 0) & (col == 1)

    @pl.when(first)
    def _():
        def greet(i, carry):
            n = lax.rem(i + 2, NR * NC)
            pl.semaphore_signal(barrier, inc=1, device_id=(n // NC, lax.rem(n, NC)), device_id_type=MESH)
            return carry

        lax.fori_loop(0, NR * NC - 1, greet, 0, unroll=7)

    loads = []
    for f, src in enumerate((heights, albedo)):
        for t in range(2):
            loads.append(
                pltpu.make_async_copy(src.at[:, pl.ds(128 * t, 128)], fields.at[f, t, pl.ds(TOP, ROWS), :], in_sem.at[2 * f + t])
            )
    load_light = pltpu.make_async_copy(lights, light, in_sem.at[4])
    load_img = [pltpu.make_async_copy(images.at[k], img.at[k], img_sem.at[k]) for k in range(NIMG)]
    load_light.start()
    for cp in load_img:
        cp.start()
    for cp in loads:
        cp.start()

    lane = lax.broadcasted_iota(jnp.int32, (8, 128), 1)
    zero = jnp.zeros((8, 128), F32)

    load_light.wait()
    lx, ly = light[0:1, :], light[1:2, :]
    inv_sq = 1.0 / (1.0 + lx * lx + ly * ly)
    inv_norm = jnp.sqrt(inv_sq)

    def over_images(x):
        return jnp.broadcast_to(jnp.sum(x, axis=1, keepdims=True), (8, 128))

    m00, m10, m01 = over_images(inv_sq), over_images(inv_sq * lx), over_images(inv_sq * ly)
    m20, m11, m02 = over_images(inv_sq * lx * lx), over_images(inv_sq * lx * ly), over_images(inv_sq * ly * ly)
    weights = [
        [jnp.broadcast_to(w[:, k : k + 1], (8, 128)) for w in (inv_norm, inv_norm * lx, inv_norm * ly)] for k in range(NIMG)
    ]

    for cp in load_img:
        cp.wait()

    def image_sums(i, carry):
        at = pl.ds(pl.multiple_of(8 * i, 8), 8)
        to = pl.ds(pl.multiple_of(8 * i + TOP, 8), 8)
        for t in range(2):
            acc = [zero, zero, zero]
            for k in range(NIMG):
                v = img[k, at, pl.ds(128 * t, 128)]
                acc = [acc[j] + weights[k][j] * v for j in range(3)]
            for j in range(3):
                fields[2 + j, t, to, :] = acc[j]
        return carry

    lax.fori_loop(0, TILES, image_sums, 0, unroll=2)
    for cp in loads:
        cp.wait()

    def tile(e):
        return pl.ds(pl.multiple_of(8 * e + 8, 8), 8)

    shifts = [(64 * g + STRIDE * f, g, f) for g in range(2) for f in range(NF)]

    def pack(j, carry):
        left, right, first = zero, zero, None
        for s, g, f in shifts:
            a = fields[f, 0, tile(j + (8 * g + 1)), :]
            b = fields[f, 1, tile(j + (8 * (1 - g) + 1)), :]
            if s:
                a, b = pltpu.roll(a, s, 1), pltpu.roll(b, s, 1)
                left = jnp.where(lane >= s, a, left)
                right = jnp.where(lane >= s - 6, b, right)
            else:
                left, right, first = a, b, b
        to = pl.ds(pl.multiple_of(8 * j, 8), 8)
        packs[0, to, :] = left
        packs[1, to, :] = jnp.where(lane >= 122, first, right)
        return carry

    lax.fori_loop(0, 8, pack, 0, unroll=4)

    @pl.when(first)
    def _():
        pl.semaphore_wait(barrier, len(peers))

    @pl.when(jnp.logical_not(first))
    def _():
        pl.semaphore_wait(barrier, len(peers) + 1)

    first8, last8 = pl.ds(0, 8), pl.ds(56, 8)
    moves = [
        (packs.at[0, first8, :], corners.at[1, 0], (-1, -1)),
        (packs.at[1, first8, :], corners.at[1, 1], (-1, 1)),
        (packs.at[0, last8, :], corners.at[0, 0], (1, -1)),
        (packs.at[1, last8, :], corners.at[0, 1], (1, 1)),
        (fields.at[:, pl.ds(0, 2), pl.ds(TOP, 8), :], rows_in.at[1], (-1, 0)),
        (fields.at[:, pl.ds(0, 2), pl.ds(TOP + ROWS - 8, 8), :], rows_in.at[0], (1, 0)),
        (packs.at[0], strips.at[0], (0, -1)),
        (packs.at[1], strips.at[1], (0, 1)),
    ]
    copies = [
        pltpu.make_async_remote_copy(
            src_ref=src, dst_ref=dst, send_sem=send_sem.at[n], recv_sem=recv_sem.at[n], device_id=dev(*to), device_id_type=MESH
        )
        for n, (src, dst, to) in enumerate(moves)
    ]
    for cp in copies:
        cp.start()

    above = jnp.where(row > 0, 1.0, 0.0).astype(F32)
    below = jnp.where(row < NR - 1, 1.0, 0.0).astype(F32)
    before = jnp.where(col > 0, 1.0, 0.0).astype(F32)
    after = jnp.where(col < NC - 1, 1.0, 0.0).astype(F32)
    side_mask = jnp.where(lane < 64, jnp.where(lane < 32, after, before), 1.0)
    is_last, is_first = lane == 127, lane == 0

    def row_mask(e):
        return jnp.where(e == 0, above, jnp.where(e == TILES + 1, below, 1.0))

    def nexts(v):
        r = [pltpu.roll(x, 127, 1) for x in v]
        return [jnp.where(is_last, r[1], r[0]), r[1]] if len(v) == 2 else r

    def prevs(v):
        r = [pltpu.roll(x, 1, 1) for x in v]
        return [r[0], jnp.where(is_first, r[0], r[1])] if len(v) == 2 else r

    def scatter(k, ts, e, q, hx, hy):
        n = nexts([a - b for a, b in zip(q, hx)])
        p = prevs([a + b for a, b in zip(q, hx)])
        for i, t in enumerate(ts):
            xs[k, t, tile(e), :] = n[i] + p[i] - 4.0 * q[i]
            yp[k, t, tile(e), :] = q[i] - hy[i]
            ym[k, t, tile(e), :] = q[i] + hy[i]

    def stencil(ref, ts, e, mask):
        v = [ref[t, tile(e), :] for t in ts]
        up = [ref[t, pl.ds(8 * e + 7, 8), :] for t in ts]
        down = [ref[t, pl.ds(8 * e + 9, 8), :] for t in ts]
        n, p = nexts(v), prevs(v)
        quarter = 0.25 if mask is None else 0.25 * mask
        q = [quarter * ((a + b) + (c + d) - 4.0 * x) for a, b, c, d, x in zip(n, p, up, down, v)]
        return v, q, [a - b for a, b in zip(n, p)], [a - b for a, b in zip(down, up)]

    def gather(k, t, e):
        return xs[k, t, tile(e), :] + yp[k, t, pl.ds(8 * e + 9, 8), :] + ym[k, t, pl.ds(8 * e + 7, 8), :]

    def mask_of(ts, e, inner):
        if inner:
            return None
        return row_mask(e) * side_mask if ts == (2,) else row_mask(e)

    def linearize(ts, inner, e):
        _, q, gx, gy = stencil(fields.at[0], ts, e, mask_of(ts, e, inner))
        hx, hy = [], []
        for i, t in enumerate(ts):
            sx, sy = 0.5 * gx[i], 0.5 * gy[i]
            inv = 1.0 / (1.0 + sx * sx + sy * sy)
            a = fields[1, t, tile(e), :] * jnp.sqrt(inv)
            j0, jx, jy = (fields[f, t, tile(e), :] for f in (2, 3, 4))
            tx, ty = sx * inv, sy * inv
            f1x = m10 - sx * m20 - sy * m11
            f1y = m01 - sx * m11 - sy * m02
            f2 = m00 - sx * m10 - sy * m01 - sx * f1x - sy * f1y
            g1x, g1y = f1x + tx * f2, f1y + ty * f2
            jf = j0 - sx * jx - sy * jy
            qa = 0.25 * (a * a)
            coef[0, t, tile(e), :] = qa * (m20 + tx * (f1x + g1x))
            coef[1, t, tile(e), :] = qa * (m11 + ty * f1x + tx * g1y)
            coef[2, t, tile(e), :] = qa * (m02 + ty * (f1y + g1y))
            ha = 0.5 * a
            hx.append(ha * (jx + tx * jf - a * g1x))
            hy.append(ha * (jy + ty * jf - a * g1y))
        scatter(0, ts, e, q, hx, hy)

    def right_side(ts, inner, e):
        m = mask_of(ts, e, inner)
        for t in ts:
            v = gather(0, t, e)
            vec_r[t, tile(e), :] = -v if m is None else -m * v

    def image_of_r(ts, inner, e):
        m = mask_of(ts, e, inner)
        for t in ts:
            v = gather(1, t, e)
            vec_u[t, tile(e), :] = v if m is None else m * v

    def weighted(ref, ts, e, mask):
        v, q, gx, gy = stencil(ref, ts, e, mask)
        cxx, cxy, cyy = ([coef[j, t, tile(e), :] for t in ts] for j in range(3))
        hx = [a * x + b * y for a, b, x, y in zip(cxx, cxy, gx, gy)]
        hy = [a * x + b * y for a, b, x, y in zip(cxy, cyy, gx, gy)]
        return v, q, gx, gy, hx, hy

    def apply_r(ts, inner, e):
        _, q, _, _, hx, hy = weighted(vec_r, ts, e, mask_of(ts, e, inner))
        scatter(1, ts, e, q, hx, hy)

    counts = {0: lane >= 8, 1: lane < 120, 2: ((lane >= 64) & (lane < 72)) | (lane >= 120)}

    def apply_u(ts, inner, e, acc, own=None):
        u, q, gx, gy, hx, hy = weighted(vec_u, ts, e, mask_of(ts, e, inner))
        scatter(2, ts, e, q, hx, hy)
        for i, t in enumerate(ts):
            ok = counts[t] if own is None else counts[t] & own
            r = vec_r[t, tile(e), :]
            terms = (r * r, r * u[i], u[i] * u[i], gx[i] * hx[i] + gy[i] * hy[i] + 4.0 * (q[i] * q[i]))
            acc = tuple(a + jnp.where(ok, x, 0.0) for a, x in zip(acc, terms))
        return acc

    def over(lo, hi, body, unroll):
        def step(e, carry):
            body(e)
            return carry

        lax.fori_loop(lo, hi, step, 0, unroll=unroll)

    main, edge = (0, 1), (2,)

    def own_edge(e):
        for f in range(NF):
            fields[f, 2, tile(e), :] = jnp.where(lane < 96, pltpu.roll(fields[f, 0, tile(e), :], 64, 1), fields[f, 1, tile(e), :])

    over(1, TILES + 1, own_edge, UN[0])
    over(1, TILES + 1, lambda e: linearize(main, True, e), UN[1])
    over(1, TILES + 1, lambda e: right_side(main, True, e), UN[1])
    over(1, TILES + 1, lambda e: apply_r(main, True, e), UN[1])
    over(1, TILES + 1, lambda e: image_of_r(main, True, e), UN[1])
    acc = lax.fori_loop(2, TILES, lambda e, acc: apply_u(main, True, e, acc), (zero, zero, zero, zero), unroll=UN[2])

    for cp in copies:
        cp.wait_recv()

    in_group = lane & 63
    from_right = in_group < 6
    for f in range(1, NF):
        from_right = from_right | ((in_group >= STRIDE * f) & (in_group < STRIDE * f + 6))

    def outer(merged, g, f):
        s = 64 * g + STRIDE * f
        return pltpu.roll(merged, 128 - s, 1) if s else merged

    def unpack(j):
        at = pl.ds(pl.multiple_of(8 * j, 8), 8)
        merged = jnp.where(from_right, strips[0, at, :], strips[1, at, :])
        for s, g, f in shifts:
            to = tile(j + (8 * g + 1))
            v = outer(merged, g, f)
            fields[f, 2, to, :] = jnp.where(lane < 64, v * side_mask if f < 2 else v, fields[f, 2, to, :])

    over(0, 8, unpack, UN[3])
    for b, g, e, ok in ((0, 1, 0, above), (1, 0, TILES + 1, below)):
        merged = jnp.where(from_right, corners[b, 0], corners[b, 1])
        for f in range(NF):
            v0, v1 = rows_in[b, f, 0], rows_in[b, f, 1]
            v = jnp.where(lane < 64, outer(merged, g, f), jnp.where(lane < 96, pltpu.roll(v0, 64, 1), v1))
            fields[f, 0, tile(e), :] = v0 * ok if f < 2 else v0
            fields[f, 1, tile(e), :] = v1 * ok if f < 2 else v1
            fields[f, 2, tile(e), :] = v * (side_mask * ok) if f < 2 else v

    def both(body):
        def step(i, carry):
            for j in range(2):
                body(main, False, TILES * i + j)
            for j in range(HALF):
                body(edge, False, HALF * i + j)
            return carry

        lax.fori_loop(0, 2, step, 0, unroll=2)

    both(linearize)
    both(right_side)
    both(apply_r)
    both(image_of_r)

    def inside(e):
        return (jnp.zeros((8, 128), jnp.int32) + e >= 1) & (jnp.zeros((8, 128), jnp.int32) + e <= TILES)

    def last(i, acc):
        for j in range(2):
            acc = apply_u(main, False, TILES * i + j, acc, inside(TILES * i + j))
        for j in range(HALF):
            acc = apply_u(edge, False, HALF * i + j, acc, inside(HALF * i + j))
        return acc

    acc = lax.fori_loop(0, 2, last, acc, unroll=2)

    folded = []
    for x in acc:
        x = x + pltpu.roll(x, 64, 1)
        folded.append(x + pltpu.roll(x, 32, 1))
    mixed = jnp.where(lane < 64, jnp.where(lane < 32, folded[0], folded[1]), jnp.where(lane < 96, folded[2], folded[3]))
    mine = jnp.sum(mixed, axis=0, keepdims=True)

    def sends(stage, slots, count, target, far):
        return [
            pltpu.make_async_remote_copy(
                src_ref=part.at[stage], dst_ref=slots.at[d - 1], send_sem=ar_send.at[stage], recv_sem=ar_recv.at[stage],
                device_id=target(d), device_id_type=MESH,
            )
            for d in sorted(range(1, count), key=lambda d: -far(d))
        ]

    def await_bytes(slots, sem):
        pltpu.make_async_copy(slots, slots, sem).wait()

    def joined(ref, e):
        side = ref[2, tile(e), :] if not isinstance(ref, int) else gather(ref, 2, e)
        inner = [ref[t, tile(e), :] if not isinstance(ref, int) else gather(ref, t, e) for t in main]
        return jnp.where(lane < 8, pltpu.roll(side, 64, 1), inner[0]), jnp.where(lane >= 120, side, inner[1])

    def merge(e):
        at = pl.ds(pl.multiple_of(8 * e - 8, 8), 8)
        for n, ref in enumerate((vec_r, vec_u, 2)):
            for t, v in enumerate(joined(ref, e)):
                krylov[n, at, pl.ds(128 * t, 128)] = v

    part[0] = mine
    direct = pltpu.make_async_remote_copy(
        src_ref=part.at[0], dst_ref=sums_all.at[row * NC + col], send_sem=ar_send.at[2], recv_sem=ar_recv.at[2],
        device_id=(0, 1), device_id_type=MESH,
    )

    @pl.when(jnp.logical_not(first))
    def _():
        direct.start()

    for cp in sends(0, sums_row, NR, lambda d: dev(d, 0), lambda d: around(d // 4, 4) + around(d, 4)):
        cp.start()
    over(1, TILES + 1, merge, 4)
    await_bytes(sums_row, ar_recv.at[0])
    total = mine
    for d in range(1, NR):
        total = total + sums_row[d - 1]
    part[1] = total

    @pl.when((row > 0) | first)
    def _():
        for cp in sends(1, sums_col, NC, lambda d: dev(0, d), lambda d: around(d, NC)):
            cp.start()

    @pl.when((row == 0) & (col != 1))
    def _():
        for d in sorted(range(1, NC), key=lambda d: -around(d, NC)):
            @pl.when(lax.rem(col + d, NC) != 1)
            def _():
                pltpu.make_async_remote_copy(
                    src_ref=part.at[1], dst_ref=sums_col.at[d - 1], send_sem=ar_send.at[1], recv_sem=ar_recv.at[1],
                    device_id=dev(0, d), device_id_type=MESH,
                ).start()

    for cp in copies:
        cp.wait_send()
    await_bytes(sums_row, ar_send.at[0])

    @pl.when(jnp.logical_not(first))
    def _():
        direct.wait_send()
        await_bytes(sums_col, ar_recv.at[1])
        total = part[1]
        for d in range(1, NC):
            total = total + sums_col[d - 1]
        part[2] = total

    @pl.when(first)
    def _():
        await_bytes(sums_all.at[pl.ds(0, NR * NC - 1)], ar_recv.at[2])
        sums_all[1] = part[0]

        def add(i, acc):
            return tuple(x + sums_all[8 * i + j] for j, x in enumerate(acc))

        acc = lax.fori_loop(0, NR * NC // 8, add, (jnp.zeros((1, 128), F32),) * 8, unroll=8)
        part[2] = ((acc[0] + acc[1]) + (acc[2] + acc[3])) + ((acc[4] + acc[5]) + (acc[6] + acc[7]))

    total = part[2]
    lane1 = lax.broadcasted_iota(jnp.int32, (1, 128), 1)

    def quarter(n):
        picked = jnp.where((lane1 >= 32 * n) & (lane1 < 32 * n + 32), total, 0.0)
        return jnp.broadcast_to(jnp.sum(picked, axis=1, keepdims=True), (8, 128))

    rr, ru, uu, uw = (quarter(n) for n in range(4))
    p1, p2, p3 = ru / rr, uu / rr, uw / rr
    step0 = 1.0 / (1.0 + p1)
    keep = p1 * step0
    beta = (p2 - p1 * p1) * (step0 * step0)
    g = keep + beta
    curve = g * g * (1.0 + p1) - 2.0 * g * step0 * (p1 + p2) + step0 * step0 * (p2 + p3)
    step1 = beta / curve
    s_r, s_u = step0 + step1 * g, -step1 * step0
    d_r, d_u, d_w = keep - step1 * g, -step0 - step1 * (g - step0), step1 * step0

    def finish(i):
        at = pl.ds(pl.multiple_of(8 * i, 8), 8)
        for t in range(2):
            lanes = pl.ds(128 * t, 128)
            r, u, w = (krylov[n, at, lanes] for n in range(3))
            out[0, at, lanes] = s_r * r + s_u * u
            out[1, at, lanes] = d_r * r + d_u * u + d_w * w

    over(0, TILES, finish, 4)

    @pl.when((row > 0) | first)
    def _():
        await_bytes(sums_col, ar_send.at[1])

    @pl.when((row == 0) & (col != 1))
    def _():
        await_bytes(sums_col.at[pl.ds(0, NC - 2)], ar_send.at[1])


def shards(heights, albedo, images, lights):
    padded = pltpu.VMEM((3, ROWS + 32, 128), F32)
    stacked = pltpu.VMEM((3, 3, ROWS + 32, 128), F32)
    out = pl.pallas_call(
        kernel,
        out_shape=jax.ShapeDtypeStruct((2, ROWS, COLS), F32),
        in_specs=[pl.BlockSpec(memory_space=pltpu.HBM)] * 4,
        out_specs=pl.BlockSpec(memory_space=pltpu.VMEM),
        scratch_shapes=[
            pltpu.VMEM((NF, 3, ROWS + 32, 128), F32),
            pltpu.VMEM((NIMG, ROWS, COLS), F32),
            pltpu.VMEM((2, NIMG), F32),
            pltpu.VMEM((2, ROWS // 2, 128), F32),
            pltpu.VMEM((2, ROWS // 2, 128), F32),
            pltpu.VMEM((2, 2, 8, 128), F32),
            pltpu.VMEM((2, NF, 2, 8, 128), F32),
            stacked,
            stacked, stacked, stacked,
            padded, padded,
            pltpu.VMEM((3, ROWS, COLS), F32),
            pltpu.VMEM((3, 1, 128), F32),
            pltpu.VMEM((NR - 1, 1, 128), F32),
            pltpu.VMEM((NC - 1, 1, 128), F32),
            pltpu.VMEM((NR * NC, 1, 128), F32),
            pltpu.SemaphoreType.DMA((5,)),
            pltpu.SemaphoreType.DMA((NIMG,)),
            pltpu.SemaphoreType.DMA((8,)),
            pltpu.SemaphoreType.DMA((8,)),
            pltpu.SemaphoreType.DMA((3,)),
            pltpu.SemaphoreType.DMA((3,)),
        ],
        compiler_params=pltpu.CompilerParams(collective_id=0, has_side_effects=True, vmem_limit_bytes=40 * 1024 * 1024),
    )(*(pltpu.with_memory_space_constraint(x, pltpu.HBM) for x in (heights, albedo, images, lights.T)))
    return out[0], out[1]


def solution(mesh):
    placed = (P("row", "col"), P("row", "col"), P(None, "row", "col"), P())
    return jax.shard_map(
        shards, mesh=mesh, in_specs=placed, out_specs=(P("row", "col"), P("row", "col")), check_vma=False
    )
```

```python
import jax
import jax.numpy as jnp
from jax import lax
from jax.experimental import pallas as pl
from jax.experimental.pallas import tpu as pltpu
from jax.sharding import PartitionSpec as P

MESH = pl.DeviceIdType.MESH
F32 = jnp.float32
NIMG = 8
NR, NC = 16, 32
ROWS, COLS = 128, 256
TILES = ROWS // 8
HALF = TILES // 2 + 1
NF = 5
TOP = 16
UN = (4, 8, 7, 8, 9)
STRIDE = 12


def around(d, count):
    return min(d % count, -d % count)


def kernel(
    heights, albedo, images, lights, out,
    fields, img, light, packs, strips, corners, rows_in, coef, xs, yp, ym, vec_r, vec_u, krylov, part, sums_row, sums_col, sums_all,
    in_sem, img_sem, send_sem, recv_sem, ar_send, ar_recv,
):
    row, col = lax.axis_index("row"), lax.axis_index("col")

    def dev(dr, dc):
        return (lax.rem(row + (dr + NR), NR), lax.rem(col + (dc + NC), NC))

    peers = {(a, b) for a in (-1, 0, 1) for b in (-1, 0, 1)} | {(d, 0) for d in range(NR)} | {(0, d) for d in range(NC)}
    peers = {(a % NR, b % NC) for a, b in peers} - {(0, 0)}
    peers = sorted(peers, key=lambda p: (p[0] == 0, -around(p[0], NR), -around(p[1], NC), p))
    barrier = pltpu.get_barrier_semaphore()
    for p in peers:
        pl.semaphore_signal(barrier, inc=1, device_id=dev(*p), device_id_type=MESH)

    first = (row == 0) & (col == 1)

    @pl.when(first)
    def _():
        def greet(i, carry):
            n = lax.rem(i + 2, NR * NC)
            pl.semaphore_signal(barrier, inc=1, device_id=(n // NC, lax.rem(n, NC)), device_id_type=MESH)
            return carry

        lax.fori_loop(0, NR * NC - 1, greet, 0, unroll=7)

    loads = []
    for f, src in enumerate((heights, albedo)):
        for t in range(2):
            loads.append(
                pltpu.make_async_copy(src.at[:, pl.ds(128 * t, 128)], fields.at[f, t, pl.ds(TOP, ROWS), :], in_sem.at[2 * f + t])
            )
    load_light = pltpu.make_async_copy(lights, light, in_sem.at[4])
    load_img = [pltpu.make_async_copy(images.at[k], img.at[k], img_sem.at[k]) for k in range(NIMG)]
    load_light.start()
    for cp in load_img:
        cp.start()
    for cp in loads:
        cp.start()

    lane = lax.broadcasted_iota(jnp.int32, (8, 128), 1)
    zero = jnp.zeros((8, 128), F32)

    load_light.wait()
    lx, ly = light[0:1, :], light[1:2, :]
    inv_sq = 1.0 / (1.0 + lx * lx + ly * ly)
    inv_norm = jnp.sqrt(inv_sq)

    def over_images(x):
        return jnp.broadcast_to(jnp.sum(x, axis=1, keepdims=True), (8, 128))

    m00, m10, m01 = over_images(inv_sq), over_images(inv_sq * lx), over_images(inv_sq * ly)
    m20, m11, m02 = over_images(inv_sq * lx * lx), over_images(inv_sq * lx * ly), over_images(inv_sq * ly * ly)
    weights = [
        [jnp.broadcast_to(w[:, k : k + 1], (8, 128)) for w in (inv_norm, inv_norm * lx, inv_norm * ly)] for k in range(NIMG)
    ]

    for cp in load_img:
        cp.wait()

    def image_sums(i, carry):
        at = pl.ds(pl.multiple_of(8 * i, 8), 8)
        to = pl.ds(pl.multiple_of(8 * i + TOP, 8), 8)
        for t in range(2):
            acc = [zero, zero, zero]
            for k in range(NIMG):
                v = img[k, at, pl.ds(128 * t, 128)]
                acc = [acc[j] + weights[k][j] * v for j in range(3)]
            for j in range(3):
                fields[2 + j, t, to, :] = acc[j]
        return carry

    lax.fori_loop(0, TILES, image_sums, 0, unroll=4)
    for cp in loads:
        cp.wait()

    def tile(e):
        return pl.ds(pl.multiple_of(8 * e + 8, 8), 8)

    shifts = [(64 * g + STRIDE * f, g, f) for g in range(2) for f in range(NF)]

    def pack(j, carry):
        left, right, first = zero, zero, None
        for s, g, f in shifts:
            a = fields[f, 0, tile(j + (8 * g + 1)), :]
            b = fields[f, 1, tile(j + (8 * (1 - g) + 1)), :]
            if s:
                a, b = pltpu.roll(a, s, 1), pltpu.roll(b, s, 1)
                left = jnp.where(lane >= s, a, left)
                right = jnp.where(lane >= s - 6, b, right)
            else:
                left, right, first = a, b, b
        to = pl.ds(pl.multiple_of(8 * j, 8), 8)
        packs[0, to, :] = left
        packs[1, to, :] = jnp.where(lane >= 122, first, right)
        return carry

    lax.fori_loop(0, 8, pack, 0, unroll=8)

    @pl.when(first)
    def _():
        pl.semaphore_wait(barrier, len(peers))

    @pl.when(jnp.logical_not(first))
    def _():
        pl.semaphore_wait(barrier, len(peers) + 1)

    first8, last8 = pl.ds(0, 8), pl.ds(56, 8)
    moves = [
        (packs.at[0, first8, :], corners.at[1, 0], (-1, -1)),
        (packs.at[1, first8, :], corners.at[1, 1], (-1, 1)),
        (packs.at[0, last8, :], corners.at[0, 0], (1, -1)),
        (packs.at[1, last8, :], corners.at[0, 1], (1, 1)),
        (fields.at[:, pl.ds(0, 2), pl.ds(TOP, 8), :], rows_in.at[1], (-1, 0)),
        (fields.at[:, pl.ds(0, 2), pl.ds(TOP + ROWS - 8, 8), :], rows_in.at[0], (1, 0)),
        (packs.at[0], strips.at[0], (0, -1)),
        (packs.at[1], strips.at[1], (0, 1)),
    ]
    copies = [
        pltpu.make_async_remote_copy(
            src_ref=src, dst_ref=dst, send_sem=send_sem.at[n], recv_sem=recv_sem.at[n], device_id=dev(*to), device_id_type=MESH
        )
        for n, (src, dst, to) in enumerate(moves)
    ]
    for cp in copies:
        cp.start()

    above = jnp.where(row > 0, 1.0, 0.0).astype(F32)
    below = jnp.where(row < NR - 1, 1.0, 0.0).astype(F32)
    before = jnp.where(col > 0, 1.0, 0.0).astype(F32)
    after = jnp.where(col < NC - 1, 1.0, 0.0).astype(F32)
    side_mask = jnp.where(lane < 64, jnp.where(lane < 32, after, before), 1.0)
    is_last, is_first = lane == 127, lane == 0

    def row_mask(e):
        return jnp.where(e == 0, above, jnp.where(e == TILES + 1, below, 1.0))

    def nexts(v):
        r = [pltpu.roll(x, 127, 1) for x in v]
        return [jnp.where(is_last, r[1], r[0]), r[1]] if len(v) == 2 else r

    def prevs(v):
        r = [pltpu.roll(x, 1, 1) for x in v]
        return [r[0], jnp.where(is_first, r[0], r[1])] if len(v) == 2 else r

    def scatter(k, ts, e, q, hx, hy):
        n = nexts([a - b for a, b in zip(q, hx)])
        p = prevs([a + b for a, b in zip(q, hx)])
        for i, t in enumerate(ts):
            xs[k, t, tile(e), :] = n[i] + p[i] - 4.0 * q[i]
            yp[k, t, tile(e), :] = q[i] - hy[i]
            ym[k, t, tile(e), :] = q[i] + hy[i]

    def stencil(ref, ts, e, mask):
        v = [ref[t, tile(e), :] for t in ts]
        up = [ref[t, pl.ds(8 * e + 7, 8), :] for t in ts]
        down = [ref[t, pl.ds(8 * e + 9, 8), :] for t in ts]
        n, p = nexts(v), prevs(v)
        quarter = 0.25 if mask is None else 0.25 * mask
        q = [quarter * ((a + b) + (c + d) - 4.0 * x) for a, b, c, d, x in zip(n, p, up, down, v)]
        return v, q, [a - b for a, b in zip(n, p)], [a - b for a, b in zip(down, up)]

    def gather(k, t, e):
        return xs[k, t, tile(e), :] + yp[k, t, pl.ds(8 * e + 9, 8), :] + ym[k, t, pl.ds(8 * e + 7, 8), :]

    def mask_of(ts, e, inner):
        if inner:
            return None
        return row_mask(e) * side_mask if ts == (2,) else row_mask(e)

    def linearize(ts, inner, e, mask=None):
        _, q, gx, gy = stencil(fields.at[0], ts, e, mask if inner else mask_of(ts, e, inner))
        hx, hy = [], []
        for i, t in enumerate(ts):
            sx, sy = 0.5 * gx[i], 0.5 * gy[i]
            inv = 1.0 / (1.0 + sx * sx + sy * sy)
            a = fields[1, t, tile(e), :] * jnp.sqrt(inv)
            j0, jx, jy = (fields[f, t, tile(e), :] for f in (2, 3, 4))
            tx, ty = sx * inv, sy * inv
            f1x = m10 - sx * m20 - sy * m11
            f1y = m01 - sx * m11 - sy * m02
            f2 = m00 - sx * m10 - sy * m01 - sx * f1x - sy * f1y
            g1x, g1y = f1x + tx * f2, f1y + ty * f2
            jf = j0 - sx * jx - sy * jy
            qa = 0.25 * (a * a)
            coef[0, t, tile(e), :] = qa * (m20 + tx * (f1x + g1x))
            coef[1, t, tile(e), :] = qa * (m11 + ty * f1x + tx * g1y)
            coef[2, t, tile(e), :] = qa * (m02 + ty * (f1y + g1y))
            ha = 0.5 * a
            hx.append(ha * (jx + tx * jf - a * g1x))
            hy.append(ha * (jy + ty * jf - a * g1y))
        scatter(0, ts, e, q, hx, hy)

    def right_side(ts, inner, e):
        m = mask_of(ts, e, inner)
        for t in ts:
            v = gather(0, t, e)
            vec_r[t, tile(e), :] = -v if m is None else -m * v

    def image_of_r(ts, inner, e):
        m = mask_of(ts, e, inner)
        for t in ts:
            v = gather(1, t, e)
            vec_u[t, tile(e), :] = v if m is None else m * v

    def weighted(ref, ts, e, mask):
        v, q, gx, gy = stencil(ref, ts, e, mask)
        cxx, cxy, cyy = ([coef[j, t, tile(e), :] for t in ts] for j in range(3))
        hx = [a * x + b * y for a, b, x, y in zip(cxx, cxy, gx, gy)]
        hy = [a * x + b * y for a, b, x, y in zip(cxy, cyy, gx, gy)]
        return v, q, gx, gy, hx, hy

    def apply_r(ts, inner, e):
        _, q, _, _, hx, hy = weighted(vec_r, ts, e, mask_of(ts, e, inner))
        scatter(1, ts, e, q, hx, hy)

    counts = {0: lane >= 8, 1: lane < 120, 2: ((lane >= 64) & (lane < 72)) | (lane >= 120)}

    def apply_u(ts, inner, e, acc, own=None):
        u, q, gx, gy, hx, hy = weighted(vec_u, ts, e, mask_of(ts, e, inner))
        scatter(2, ts, e, q, hx, hy)
        for i, t in enumerate(ts):
            ok = counts[t] if own is None else counts[t] & own
            r = vec_r[t, tile(e), :]
            terms = (r * r, r * u[i], u[i] * u[i], gx[i] * hx[i] + gy[i] * hy[i] + 4.0 * (q[i] * q[i]))
            acc = tuple(a + jnp.where(ok, x, 0.0) for a, x in zip(acc, terms))
        return acc

    def over(lo, hi, body, unroll):
        def step(e, carry):
            body(e)
            return carry

        lax.fori_loop(lo, hi, step, 0, unroll=unroll)

    main, edge = (0, 1), (2,)

    def own_edge(e):
        for f in range(NF):
            fields[f, 2, tile(e), :] = jnp.where(lane < 96, pltpu.roll(fields[f, 0, tile(e), :], 64, 1), fields[f, 1, tile(e), :])

    over(1, TILES + 1, own_edge, UN[0])
    over(1, TILES + 1, lambda e: linearize(main, True, e), UN[1])
    over(1, TILES + 1, lambda e: right_side(main, True, e), UN[1])
    over(1, TILES + 1, lambda e: apply_r(main, True, e), UN[1])
    over(1, TILES + 1, lambda e: image_of_r(main, True, e), UN[1])
    acc = lax.fori_loop(2, TILES, lambda e, acc: apply_u(main, True, e, acc), (zero, zero, zero, zero), unroll=UN[2])

    for cp in copies[6:]:
        cp.wait_recv()

    in_group = lane & 63
    from_right = in_group < 6
    for f in range(1, NF):
        from_right = from_right | ((in_group >= STRIDE * f) & (in_group < STRIDE * f + 6))

    def outer(merged, g, f):
        s = 64 * g + STRIDE * f
        return pltpu.roll(merged, 128 - s, 1) if s else merged

    def unpack(j):
        at = pl.ds(pl.multiple_of(8 * j, 8), 8)
        merged = jnp.where(from_right, strips[0, at, :], strips[1, at, :])
        for s, g, f in shifts:
            to = tile(j + (8 * g + 1))
            v = outer(merged, g, f)
            fields[f, 2, to, :] = jnp.where(lane < 64, v * side_mask if f < 2 else v, fields[f, 2, to, :])

    over(0, 8, unpack, UN[3])
    over(2, TILES, lambda e: linearize(edge, True, e, side_mask), TILES - 2)
    for cp in copies[:6]:
        cp.wait_recv()
    for b, g, e, ok in ((0, 1, 0, above), (1, 0, TILES + 1, below)):
        merged = jnp.where(from_right, corners[b, 0], corners[b, 1])
        for f in range(NF):
            v0, v1 = rows_in[b, f, 0], rows_in[b, f, 1]
            v = jnp.where(lane < 64, outer(merged, g, f), jnp.where(lane < 96, pltpu.roll(v0, 64, 1), v1))
            fields[f, 0, tile(e), :] = v0 * ok if f < 2 else v0
            fields[f, 1, tile(e), :] = v1 * ok if f < 2 else v1
            fields[f, 2, tile(e), :] = v * (side_mask * ok) if f < 2 else v

    def both(body):
        def step(i, carry):
            for j in range(2):
                body(main, False, TILES * i + j)
            for j in range(HALF):
                body(edge, False, HALF * i + j)
            return carry

        lax.fori_loop(0, 2, step, 0, unroll=2)

    def linearize_rows(i, carry):
        for j in range(2):
            linearize(main, False, TILES * i + j)
            linearize(edge, False, TILES * i + j)
        return carry

    lax.fori_loop(0, 2, linearize_rows, 0, unroll=2)
    both(right_side)
    both(apply_r)
    both(image_of_r)

    def inside(e):
        return (jnp.zeros((8, 128), jnp.int32) + e >= 1) & (jnp.zeros((8, 128), jnp.int32) + e <= TILES)

    def last(i, acc):
        for j in range(2):
            acc = apply_u(main, False, TILES * i + j, acc, inside(TILES * i + j))
        for j in range(HALF):
            acc = apply_u(edge, False, HALF * i + j, acc, inside(HALF * i + j))
        return acc

    acc = lax.fori_loop(0, 2, last, acc, unroll=2)

    folded = []
    for x in acc:
        x = x + pltpu.roll(x, 64, 1)
        folded.append(x + pltpu.roll(x, 32, 1))
    mixed = jnp.where(lane < 64, jnp.where(lane < 32, folded[0], folded[1]), jnp.where(lane < 96, folded[2], folded[3]))
    mine = jnp.sum(mixed, axis=0, keepdims=True)

    def sends(stage, slots, count, target, far):
        return [
            pltpu.make_async_remote_copy(
                src_ref=part.at[stage], dst_ref=slots.at[d - 1], send_sem=ar_send.at[stage], recv_sem=ar_recv.at[stage],
                device_id=target(d), device_id_type=MESH,
            )
            for d in sorted(range(1, count), key=lambda d: -far(d))
        ]

    def await_bytes(slots, sem):
        pltpu.make_async_copy(slots, slots, sem).wait()

    def joined(ref, e):
        side = ref[2, tile(e), :] if not isinstance(ref, int) else gather(ref, 2, e)
        inner = [ref[t, tile(e), :] if not isinstance(ref, int) else gather(ref, t, e) for t in main]
        return jnp.where(lane < 8, pltpu.roll(side, 64, 1), inner[0]), jnp.where(lane >= 120, side, inner[1])

    def merge(e):
        at = pl.ds(pl.multiple_of(8 * e - 8, 8), 8)
        for n, ref in enumerate((vec_r, vec_u, 2)):
            for t, v in enumerate(joined(ref, e)):
                krylov[n, at, pl.ds(128 * t, 128)] = v

    part[0] = mine
    direct = pltpu.make_async_remote_copy(
        src_ref=part.at[0], dst_ref=sums_all.at[row * NC + col], send_sem=ar_send.at[2], recv_sem=ar_recv.at[2],
        device_id=(0, 1), device_id_type=MESH,
    )

    @pl.when(jnp.logical_not(first))
    def _():
        direct.start()

    for cp in sends(0, sums_row, NR, lambda d: dev(d, 0), lambda d: around(d // 4, 4) + around(d, 4)):
        cp.start()
    over(1, TILES + 1, merge, 4)
    await_bytes(sums_row, ar_recv.at[0])
    total = mine
    for d in range(1, NR):
        total = total + sums_row[d - 1]
    part[1] = total

    @pl.when((row > 0) | first)
    def _():
        for cp in sends(1, sums_col, NC, lambda d: dev(0, d), lambda d: around(d, NC)):
            cp.start()

    @pl.when((row == 0) & (col != 1))
    def _():
        for d in sorted(range(1, NC), key=lambda d: -around(d, NC)):
            @pl.when(lax.rem(col + d, NC) != 1)
            def _():
                pltpu.make_async_remote_copy(
                    src_ref=part.at[1], dst_ref=sums_col.at[d - 1], send_sem=ar_send.at[1], recv_sem=ar_recv.at[1],
                    device_id=dev(0, d), device_id_type=MESH,
                ).start()

    for cp in copies:
        cp.wait_send()
    await_bytes(sums_row, ar_send.at[0])

    @pl.when(jnp.logical_not(first))
    def _():
        direct.wait_send()
        await_bytes(sums_col, ar_recv.at[1])
        total = part[1]
        for d in range(1, NC):
            total = total + sums_col[d - 1]
        part[2] = total

    @pl.when(first)
    def _():
        await_bytes(sums_all.at[pl.ds(0, NR * NC - 1)], ar_recv.at[2])
        sums_all[1] = part[0]

        def add(i, acc):
            return tuple(x + sums_all[8 * i + j] for j, x in enumerate(acc))

        acc = lax.fori_loop(0, NR * NC // 8, add, (jnp.zeros((1, 128), F32),) * 8, unroll=8)
        part[2] = ((acc[0] + acc[1]) + (acc[2] + acc[3])) + ((acc[4] + acc[5]) + (acc[6] + acc[7]))

    total = part[2]
    lane1 = lax.broadcasted_iota(jnp.int32, (1, 128), 1)

    def quarter(n):
        picked = jnp.where((lane1 >= 32 * n) & (lane1 < 32 * n + 32), total, 0.0)
        return jnp.broadcast_to(jnp.sum(picked, axis=1, keepdims=True), (8, 128))

    rr, ru, uu, uw = (quarter(n) for n in range(4))
    p1, p2, p3 = ru / rr, uu / rr, uw / rr
    step0 = 1.0 / (1.0 + p1)
    keep = p1 * step0
    beta = (p2 - p1 * p1) * (step0 * step0)
    g = keep + beta
    curve = g * g * (1.0 + p1) - 2.0 * g * step0 * (p1 + p2) + step0 * step0 * (p2 + p3)
    step1 = beta / curve
    s_r, s_u = step0 + step1 * g, -step1 * step0
    d_r, d_u, d_w = keep - step1 * g, -step0 - step1 * (g - step0), step1 * step0

    def finish(i):
        at = pl.ds(pl.multiple_of(8 * i, 8), 8)
        for t in range(2):
            lanes = pl.ds(128 * t, 128)
            r, u, w = (krylov[n, at, lanes] for n in range(3))
            out[0, at, lanes] = s_r * r + s_u * u
            out[1, at, lanes] = d_r * r + d_u * u + d_w * w

    over(0, TILES, finish, 16)

    @pl.when((row > 0) | first)
    def _():
        await_bytes(sums_col, ar_send.at[1])

    @pl.when((row == 0) & (col != 1))
    def _():
        await_bytes(sums_col.at[pl.ds(0, NC - 2)], ar_send.at[1])


def shards(heights, albedo, images, lights):
    padded = pltpu.VMEM((3, ROWS + 32, 128), F32)
    stacked = pltpu.VMEM((3, 3, ROWS + 32, 128), F32)
    out = pl.pallas_call(
        kernel,
        out_shape=jax.ShapeDtypeStruct((2, ROWS, COLS), F32),
        in_specs=[pl.BlockSpec(memory_space=pltpu.HBM)] * 4,
        out_specs=pl.BlockSpec(memory_space=pltpu.VMEM),
        scratch_shapes=[
            pltpu.VMEM((NF, 3, ROWS + 32, 128), F32),
            pltpu.VMEM((NIMG, ROWS, COLS), F32),
            pltpu.VMEM((2, NIMG), F32),
            pltpu.VMEM((2, ROWS // 2, 128), F32),
            pltpu.VMEM((2, ROWS // 2, 128), F32),
            pltpu.VMEM((2, 2, 8, 128), F32),
            pltpu.VMEM((2, NF, 2, 8, 128), F32),
            stacked,
            stacked, stacked, stacked,
            padded, padded,
            pltpu.VMEM((3, ROWS, COLS), F32),
            pltpu.VMEM((3, 1, 128), F32),
            pltpu.VMEM((NR - 1, 1, 128), F32),
            pltpu.VMEM((NC - 1, 1, 128), F32),
            pltpu.VMEM((NR * NC, 1, 128), F32),
            pltpu.SemaphoreType.DMA((5,)),
            pltpu.SemaphoreType.DMA((NIMG,)),
            pltpu.SemaphoreType.DMA((8,)),
            pltpu.SemaphoreType.DMA((8,)),
            pltpu.SemaphoreType.DMA((3,)),
            pltpu.SemaphoreType.DMA((3,)),
        ],
        compiler_params=pltpu.CompilerParams(collective_id=0, has_side_effects=True, vmem_limit_bytes=40 * 1024 * 1024),
    )(*(pltpu.with_memory_space_constraint(x, pltpu.HBM) for x in (heights, albedo, images, lights.T)))
    return out[0], out[1]


def solution(mesh):
    placed = (P("row", "col"), P("row", "col"), P(None, "row", "col"), P())
    return jax.shard_map(
        shards, mesh=mesh, in_specs=placed, out_specs=(P("row", "col"), P("row", "col")), check_vma=False
    )
```

```python
import jax
import jax.numpy as jnp
from jax import lax
from jax.experimental import pallas as pl
from jax.experimental.pallas import tpu as pltpu
from jax.sharding import PartitionSpec as P

MESH = pl.DeviceIdType.MESH
F32 = jnp.float32
NIMG = 8
NR, NC = 16, 32
ROWS, COLS = 128, 256
TILES = ROWS // 8
HALF = TILES // 2 + 1
NF = 5
TOP = 16
UN = (4, 8, 7, 8, 9)
STRIDE = 12


def around(d, count):
    return min(d % count, -d % count)


def kernel(
    heights, albedo, images, lights, out,
    fields, img, light, packs, strips, corners, rows_in, coef, xs, yp, ym, vec_r, vec_u, krylov, part, sums_row, sums_col, sums_all,
    in_sem, img_sem, send_sem, recv_sem, ar_send, ar_recv,
):
    row, col = lax.axis_index("row"), lax.axis_index("col")

    def dev(dr, dc):
        return (lax.rem(row + (dr + NR), NR), lax.rem(col + (dc + NC), NC))

    peers = {(a, b) for a in (-1, 0, 1) for b in (-1, 0, 1)} | {(d, 0) for d in range(NR)} | {(0, d) for d in range(NC)}
    peers = {(a % NR, b % NC) for a, b in peers} - {(0, 0)}
    peers = sorted(peers, key=lambda p: (p[0] == 0, -around(p[0], NR), -around(p[1], NC), p))
    barrier = pltpu.get_barrier_semaphore()
    for p in peers:
        pl.semaphore_signal(barrier, inc=1, device_id=dev(*p), device_id_type=MESH)

    first = (row == 0) & (col == 1)

    @pl.when(first)
    def _():
        def greet(i, carry):
            n = lax.rem(i + 2, NR * NC)
            pl.semaphore_signal(barrier, inc=1, device_id=(n // NC, lax.rem(n, NC)), device_id_type=MESH)
            return carry

        lax.fori_loop(0, NR * NC - 1, greet, 0, unroll=7)

    loads = []
    for f, src in enumerate((heights, albedo)):
        for t in range(2):
            loads.append(
                pltpu.make_async_copy(src.at[:, pl.ds(128 * t, 128)], fields.at[f, t, pl.ds(TOP, ROWS), :], in_sem.at[2 * f + t])
            )
    load_light = pltpu.make_async_copy(lights, light, in_sem.at[4])
    load_img = [pltpu.make_async_copy(images.at[k], img.at[k], img_sem.at[k]) for k in range(NIMG)]
    load_light.start()
    for cp in load_img:
        cp.start()
    for cp in loads:
        cp.start()

    lane = lax.broadcasted_iota(jnp.int32, (8, 128), 1)
    zero = jnp.zeros((8, 128), F32)

    load_light.wait()
    lx, ly = light[0:1, :], light[1:2, :]
    inv_sq = 1.0 / (1.0 + lx * lx + ly * ly)
    inv_norm = jnp.sqrt(inv_sq)

    def over_images(x):
        return jnp.broadcast_to(jnp.sum(x, axis=1, keepdims=True), (8, 128))

    m00, m10, m01 = over_images(inv_sq), over_images(inv_sq * lx), over_images(inv_sq * ly)
    m20, m11, m02 = over_images(inv_sq * lx * lx), over_images(inv_sq * lx * ly), over_images(inv_sq * ly * ly)
    weights = [
        [jnp.broadcast_to(w[:, k : k + 1], (8, 128)) for w in (inv_norm, inv_norm * lx, inv_norm * ly)] for k in range(NIMG)
    ]

    for cp in load_img:
        cp.wait()

    def image_sums(i, carry):
        at = pl.ds(pl.multiple_of(8 * i, 8), 8)
        to = pl.ds(pl.multiple_of(8 * i + TOP, 8), 8)
        for t in range(2):
            acc = [zero, zero, zero]
            for k in range(NIMG):
                v = img[k, at, pl.ds(128 * t, 128)]
                acc = [acc[j] + weights[k][j] * v for j in range(3)]
            for j in range(3):
                fields[2 + j, t, to, :] = acc[j]
        return carry

    lax.fori_loop(0, TILES, image_sums, 0, unroll=4)
    for cp in loads:
        cp.wait()

    def tile(e):
        return pl.ds(pl.multiple_of(8 * e + 8, 8), 8)

    shifts = [(64 * g + STRIDE * f, g, f) for g in range(2) for f in range(NF)]

    def pack(j, carry):
        left, right, first = zero, zero, None
        for s, g, f in shifts:
            a = fields[f, 0, tile(j + (8 * g + 1)), :]
            b = fields[f, 1, tile(j + (8 * (1 - g) + 1)), :]
            if s:
                a, b = pltpu.roll(a, s, 1), pltpu.roll(b, s, 1)
                left = jnp.where(lane >= s, a, left)
                right = jnp.where(lane >= s - 6, b, right)
            else:
                left, right, first = a, b, b
        to = pl.ds(pl.multiple_of(8 * j, 8), 8)
        packs[0, to, :] = left
        packs[1, to, :] = jnp.where(lane >= 122, first, right)
        return carry

    lax.fori_loop(0, 8, pack, 0, unroll=8)

    @pl.when(first)
    def _():
        pl.semaphore_wait(barrier, len(peers))

    @pl.when(jnp.logical_not(first))
    def _():
        pl.semaphore_wait(barrier, len(peers) + 1)

    first8, last8 = pl.ds(0, 8), pl.ds(56, 8)
    moves = [
        (packs.at[0, first8, :], corners.at[1, 0], (-1, -1)),
        (packs.at[1, first8, :], corners.at[1, 1], (-1, 1)),
        (packs.at[0, last8, :], corners.at[0, 0], (1, -1)),
        (packs.at[1, last8, :], corners.at[0, 1], (1, 1)),
        (fields.at[:, pl.ds(0, 2), pl.ds(TOP, 8), :], rows_in.at[1], (-1, 0)),
        (fields.at[:, pl.ds(0, 2), pl.ds(TOP + ROWS - 8, 8), :], rows_in.at[0], (1, 0)),
        (packs.at[0], strips.at[0], (0, -1)),
        (packs.at[1], strips.at[1], (0, 1)),
    ]
    copies = [
        pltpu.make_async_remote_copy(
            src_ref=src, dst_ref=dst, send_sem=send_sem.at[n], recv_sem=recv_sem.at[n], device_id=dev(*to), device_id_type=MESH
        )
        for n, (src, dst, to) in enumerate(moves)
    ]
    for n in (4, 5, 0, 1, 2, 3, 6, 7):
        copies[n].start()

    above = jnp.where(row > 0, 1.0, 0.0).astype(F32)
    below = jnp.where(row < NR - 1, 1.0, 0.0).astype(F32)
    before = jnp.where(col > 0, 1.0, 0.0).astype(F32)
    after = jnp.where(col < NC - 1, 1.0, 0.0).astype(F32)
    side_mask = jnp.where(lane < 64, jnp.where(lane < 32, after, before), 1.0)
    is_last, is_first = lane == 127, lane == 0

    def row_mask(e):
        return jnp.where(e == 0, above, jnp.where(e == TILES + 1, below, 1.0))

    def nexts(v):
        r = [pltpu.roll(x, 127, 1) for x in v]
        return [jnp.where(is_last, r[1], r[0]), r[1]] if len(v) == 2 else r

    def prevs(v):
        r = [pltpu.roll(x, 1, 1) for x in v]
        return [r[0], jnp.where(is_first, r[0], r[1])] if len(v) == 2 else r

    def scatter(k, ts, e, q, hx, hy):
        n = nexts([a - b for a, b in zip(q, hx)])
        p = prevs([a + b for a, b in zip(q, hx)])
        for i, t in enumerate(ts):
            xs[k, t, tile(e), :] = n[i] + p[i] - 4.0 * q[i]
            yp[k, t, tile(e), :] = q[i] - hy[i]
            ym[k, t, tile(e), :] = q[i] + hy[i]

    def stencil(ref, ts, e, mask):
        v = [ref[t, tile(e), :] for t in ts]
        up = [ref[t, pl.ds(8 * e + 7, 8), :] for t in ts]
        down = [ref[t, pl.ds(8 * e + 9, 8), :] for t in ts]
        n, p = nexts(v), prevs(v)
        quarter = 0.25 if mask is None else 0.25 * mask
        q = [quarter * ((a + b) + (c + d) - 4.0 * x) for a, b, c, d, x in zip(n, p, up, down, v)]
        return v, q, [a - b for a, b in zip(n, p)], [a - b for a, b in zip(down, up)]

    def gather(k, t, e):
        return xs[k, t, tile(e), :] + yp[k, t, pl.ds(8 * e + 9, 8), :] + ym[k, t, pl.ds(8 * e + 7, 8), :]

    def mask_of(ts, e, inner):
        if inner:
            return None
        return row_mask(e) * side_mask if ts == (2,) else row_mask(e)

    def linearize(ts, inner, e, mask=None):
        _, q, gx, gy = stencil(fields.at[0], ts, e, mask if inner else mask_of(ts, e, inner))
        hx, hy = [], []
        for i, t in enumerate(ts):
            sx, sy = 0.5 * gx[i], 0.5 * gy[i]
            inv = 1.0 / (1.0 + sx * sx + sy * sy)
            a = fields[1, t, tile(e), :] * jnp.sqrt(inv)
            j0, jx, jy = (fields[f, t, tile(e), :] for f in (2, 3, 4))
            tx, ty = sx * inv, sy * inv
            f1x = m10 - sx * m20 - sy * m11
            f1y = m01 - sx * m11 - sy * m02
            f2 = m00 - sx * m10 - sy * m01 - sx * f1x - sy * f1y
            g1x, g1y = f1x + tx * f2, f1y + ty * f2
            jf = j0 - sx * jx - sy * jy
            qa = 0.25 * (a * a)
            coef[0, t, tile(e), :] = qa * (m20 + tx * (f1x + g1x))
            coef[1, t, tile(e), :] = qa * (m11 + ty * f1x + tx * g1y)
            coef[2, t, tile(e), :] = qa * (m02 + ty * (f1y + g1y))
            ha = 0.5 * a
            hx.append(ha * (jx + tx * jf - a * g1x))
            hy.append(ha * (jy + ty * jf - a * g1y))
        scatter(0, ts, e, q, hx, hy)

    def right_side(ts, inner, e):
        m = mask_of(ts, e, inner)
        for t in ts:
            v = gather(0, t, e)
            vec_r[t, tile(e), :] = -v if m is None else -m * v

    def image_of_r(ts, inner, e):
        m = mask_of(ts, e, inner)
        for t in ts:
            v = gather(1, t, e)
            vec_u[t, tile(e), :] = v if m is None else m * v

    def weighted(ref, ts, e, mask):
        v, q, gx, gy = stencil(ref, ts, e, mask)
        cxx, cxy, cyy = ([coef[j, t, tile(e), :] for t in ts] for j in range(3))
        hx = [a * x + b * y for a, b, x, y in zip(cxx, cxy, gx, gy)]
        hy = [a * x + b * y for a, b, x, y in zip(cxy, cyy, gx, gy)]
        return v, q, gx, gy, hx, hy

    def apply_r(ts, inner, e):
        _, q, _, _, hx, hy = weighted(vec_r, ts, e, mask_of(ts, e, inner))
        scatter(1, ts, e, q, hx, hy)

    counts = {0: lane >= 8, 1: lane < 120, 2: ((lane >= 64) & (lane < 72)) | (lane >= 120)}

    def apply_u(ts, inner, e, acc, own=None):
        u, q, gx, gy, hx, hy = weighted(vec_u, ts, e, mask_of(ts, e, inner))
        scatter(2, ts, e, q, hx, hy)
        for i, t in enumerate(ts):
            ok = counts[t] if own is None else counts[t] & own
            r = vec_r[t, tile(e), :]
            terms = (r * r, r * u[i], u[i] * u[i], gx[i] * hx[i] + gy[i] * hy[i] + 4.0 * (q[i] * q[i]))
            acc = tuple(a + jnp.where(ok, x, 0.0) for a, x in zip(acc, terms))
        return acc

    def over(lo, hi, body, unroll):
        def step(e, carry):
            body(e)
            return carry

        lax.fori_loop(lo, hi, step, 0, unroll=unroll)

    main, edge = (0, 1), (2,)

    def own_edge(e):
        for f in range(NF):
            fields[f, 2, tile(e), :] = jnp.where(lane < 96, pltpu.roll(fields[f, 0, tile(e), :], 64, 1), fields[f, 1, tile(e), :])

    over(1, TILES + 1, own_edge, UN[0])
    over(1, TILES + 1, lambda e: linearize(main, True, e), UN[1])
    over(1, TILES + 1, lambda e: right_side(main, True, e), UN[1])
    over(1, TILES + 1, lambda e: apply_r(main, True, e), UN[1])
    over(1, TILES + 1, lambda e: image_of_r(main, True, e), UN[1])
    acc = lax.fori_loop(2, TILES, lambda e, acc: apply_u(main, True, e, acc), (zero, zero, zero, zero), unroll=UN[2])

    for cp in copies[6:]:
        cp.wait_recv()

    in_group = lane & 63
    from_right = in_group < 6
    for f in range(1, NF):
        from_right = from_right | ((in_group >= STRIDE * f) & (in_group < STRIDE * f + 6))

    def outer(merged, g, f):
        s = 64 * g + STRIDE * f
        return pltpu.roll(merged, 128 - s, 1) if s else merged

    def unpack(j):
        at = pl.ds(pl.multiple_of(8 * j, 8), 8)
        merged = jnp.where(from_right, strips[0, at, :], strips[1, at, :])
        for s, g, f in shifts:
            to = tile(j + (8 * g + 1))
            v = outer(merged, g, f)
            fields[f, 2, to, :] = jnp.where(lane < 64, v * side_mask if f < 2 else v, fields[f, 2, to, :])

    over(0, 8, unpack, UN[3])
    over(2, TILES, lambda e: linearize(edge, True, e, side_mask), TILES - 2)
    for cp in copies[:6]:
        cp.wait_recv()
    for b, g, e, ok in ((0, 1, 0, above), (1, 0, TILES + 1, below)):
        merged = jnp.where(from_right, corners[b, 0], corners[b, 1])
        for f in range(NF):
            v0, v1 = rows_in[b, f, 0], rows_in[b, f, 1]
            v = jnp.where(lane < 64, outer(merged, g, f), jnp.where(lane < 96, pltpu.roll(v0, 64, 1), v1))
            fields[f, 0, tile(e), :] = v0 * ok if f < 2 else v0
            fields[f, 1, tile(e), :] = v1 * ok if f < 2 else v1
            fields[f, 2, tile(e), :] = v * (side_mask * ok) if f < 2 else v

    def both(body):
        def step(i, carry):
            for j in range(2):
                body(main, False, TILES * i + j)
            for j in range(HALF):
                body(edge, False, HALF * i + j)
            return carry

        lax.fori_loop(0, 2, step, 0, unroll=2)

    def linearize_rows(i, carry):
        for j in range(2):
            linearize(main, False, TILES * i + j)
            linearize(edge, False, TILES * i + j)
        return carry

    lax.fori_loop(0, 2, linearize_rows, 0, unroll=2)
    both(right_side)
    both(apply_r)
    both(image_of_r)

    def inside(e):
        return (jnp.zeros((8, 128), jnp.int32) + e >= 1) & (jnp.zeros((8, 128), jnp.int32) + e <= TILES)

    def last(i, acc):
        for j in range(2):
            acc = apply_u(main, False, TILES * i + j, acc, inside(TILES * i + j))
        for j in range(HALF):
            acc = apply_u(edge, False, HALF * i + j, acc, inside(HALF * i + j))
        return acc

    acc = lax.fori_loop(0, 2, last, acc, unroll=2)

    folded = []
    for x in acc:
        x = x + pltpu.roll(x, 64, 1)
        folded.append(x + pltpu.roll(x, 32, 1))
    mixed = jnp.where(lane < 64, jnp.where(lane < 32, folded[0], folded[1]), jnp.where(lane < 96, folded[2], folded[3]))
    mine = jnp.sum(mixed, axis=0, keepdims=True)

    def sends(stage, slots, count, target, far):
        return [
            pltpu.make_async_remote_copy(
                src_ref=part.at[stage], dst_ref=slots.at[d - 1], send_sem=ar_send.at[stage], recv_sem=ar_recv.at[stage],
                device_id=target(d), device_id_type=MESH,
            )
            for d in sorted(range(1, count), key=lambda d: -far(d))
        ]

    def await_bytes(slots, sem):
        pltpu.make_async_copy(slots, slots, sem).wait()

    def joined(ref, e):
        side = ref[2, tile(e), :] if not isinstance(ref, int) else gather(ref, 2, e)
        inner = [ref[t, tile(e), :] if not isinstance(ref, int) else gather(ref, t, e) for t in main]
        return jnp.where(lane < 8, pltpu.roll(side, 64, 1), inner[0]), jnp.where(lane >= 120, side, inner[1])

    def merge(e):
        at = pl.ds(pl.multiple_of(8 * e - 8, 8), 8)
        for n, ref in enumerate((vec_r, vec_u, 2)):
            for t, v in enumerate(joined(ref, e)):
                krylov[n, at, pl.ds(128 * t, 128)] = v

    part[0] = mine
    direct = pltpu.make_async_remote_copy(
        src_ref=part.at[0], dst_ref=sums_all.at[row * NC + col], send_sem=ar_send.at[2], recv_sem=ar_recv.at[2],
        device_id=(0, 1), device_id_type=MESH,
    )

    @pl.when(jnp.logical_not(first))
    def _():
        direct.start()

    for cp in sends(0, sums_row, NR, lambda d: dev(d, 0), lambda d: around(d // 4, 4) + around(d, 4)):
        cp.start()
    over(1, TILES + 1, merge, 4)
    await_bytes(sums_row, ar_recv.at[0])
    total = mine
    for d in range(1, NR):
        total = total + sums_row[d - 1]
    part[1] = total

    @pl.when((row > 0) | first)
    def _():
        for cp in sends(1, sums_col, NC, lambda d: dev(0, d), lambda d: around(d, NC)):
            cp.start()

    @pl.when((row == 0) & (col != 1))
    def _():
        for d in sorted(range(1, NC), key=lambda d: -around(d, NC)):
            @pl.when(lax.rem(col + d, NC) != 1)
            def _():
                pltpu.make_async_remote_copy(
                    src_ref=part.at[1], dst_ref=sums_col.at[d - 1], send_sem=ar_send.at[1], recv_sem=ar_recv.at[1],
                    device_id=dev(0, d), device_id_type=MESH,
                ).start()

    for cp in copies:
        cp.wait_send()
    await_bytes(sums_row, ar_send.at[0])

    @pl.when(jnp.logical_not(first))
    def _():
        direct.wait_send()
        await_bytes(sums_col, ar_recv.at[1])
        total = part[1]
        for d in range(1, NC):
            total = total + sums_col[d - 1]
        part[2] = total

    @pl.when(first)
    def _():
        await_bytes(sums_all.at[pl.ds(0, NR * NC - 1)], ar_recv.at[2])
        sums_all[1] = part[0]

        def add(i, acc):
            return tuple(x + sums_all[8 * i + j] for j, x in enumerate(acc))

        acc = lax.fori_loop(0, NR * NC // 8, add, (jnp.zeros((1, 128), F32),) * 8, unroll=8)
        part[2] = ((acc[0] + acc[1]) + (acc[2] + acc[3])) + ((acc[4] + acc[5]) + (acc[6] + acc[7]))

    total = part[2]
    lane1 = lax.broadcasted_iota(jnp.int32, (1, 128), 1)

    def quarter(n):
        picked = jnp.where((lane1 >= 32 * n) & (lane1 < 32 * n + 32), total, 0.0)
        return jnp.broadcast_to(jnp.sum(picked, axis=1, keepdims=True), (8, 128))

    rr, ru, uu, uw = (quarter(n) for n in range(4))
    p1, p2, p3 = ru / rr, uu / rr, uw / rr
    step0 = 1.0 / (1.0 + p1)
    keep = p1 * step0
    beta = (p2 - p1 * p1) * (step0 * step0)
    g = keep + beta
    curve = g * g * (1.0 + p1) - 2.0 * g * step0 * (p1 + p2) + step0 * step0 * (p2 + p3)
    step1 = beta / curve
    s_r, s_u = step0 + step1 * g, -step1 * step0
    d_r, d_u, d_w = keep - step1 * g, -step0 - step1 * (g - step0), step1 * step0

    def finish(i):
        at = pl.ds(pl.multiple_of(8 * i, 8), 8)
        for t in range(2):
            lanes = pl.ds(128 * t, 128)
            r, u, w = (krylov[n, at, lanes] for n in range(3))
            out[0, at, lanes] = s_r * r + s_u * u
            out[1, at, lanes] = d_r * r + d_u * u + d_w * w

    over(0, TILES, finish, 16)

    @pl.when((row > 0) | first)
    def _():
        await_bytes(sums_col, ar_send.at[1])

    @pl.when((row == 0) & (col != 1))
    def _():
        await_bytes(sums_col.at[pl.ds(0, NC - 2)], ar_send.at[1])


def shards(heights, albedo, images, lights):
    padded = pltpu.VMEM((3, ROWS + 32, 128), F32)
    stacked = pltpu.VMEM((3, 3, ROWS + 32, 128), F32)
    out = pl.pallas_call(
        kernel,
        out_shape=jax.ShapeDtypeStruct((2, ROWS, COLS), F32),
        in_specs=[pl.BlockSpec(memory_space=pltpu.HBM)] * 4,
        out_specs=pl.BlockSpec(memory_space=pltpu.VMEM),
        scratch_shapes=[
            pltpu.VMEM((NF, 3, ROWS + 32, 128), F32),
            pltpu.VMEM((NIMG, ROWS, COLS), F32),
            pltpu.VMEM((2, NIMG), F32),
            pltpu.VMEM((2, ROWS // 2, 128), F32),
            pltpu.VMEM((2, ROWS // 2, 128), F32),
            pltpu.VMEM((2, 2, 8, 128), F32),
            pltpu.VMEM((2, NF, 2, 8, 128), F32),
            stacked,
            stacked, stacked, stacked,
            padded, padded,
            pltpu.VMEM((3, ROWS, COLS), F32),
            pltpu.VMEM((3, 1, 128), F32),
            pltpu.VMEM((NR - 1, 1, 128), F32),
            pltpu.VMEM((NC - 1, 1, 128), F32),
            pltpu.VMEM((NR * NC, 1, 128), F32),
            pltpu.SemaphoreType.DMA((5,)),
            pltpu.SemaphoreType.DMA((NIMG,)),
            pltpu.SemaphoreType.DMA((8,)),
            pltpu.SemaphoreType.DMA((8,)),
            pltpu.SemaphoreType.DMA((3,)),
            pltpu.SemaphoreType.DMA((3,)),
        ],
        compiler_params=pltpu.CompilerParams(collective_id=0, has_side_effects=True, vmem_limit_bytes=40 * 1024 * 1024),
    )(*(pltpu.with_memory_space_constraint(x, pltpu.HBM) for x in (heights, albedo, images, lights.T)))
    return out[0], out[1]


def solution(mesh):
    placed = (P("row", "col"), P("row", "col"), P(None, "row", "col"), P())
    return jax.shard_map(
        shards, mesh=mesh, in_specs=placed, out_specs=(P("row", "col"), P("row", "col")), check_vma=False
    )
```
